32 devices in a mesh: grp: 2 (over x), orb: 16 (over z, y, core).
Axes of the slice: x: 2, y: 2, z: 4, core: 2. Of those that a mesh axis runs over, the one named last changes fastest.
Arguments:
- tensor: bfloat16 [128, 2048, 384], P('grp', 'orb'), parts along dimension 0, may hold values from -0.25 to 0.25
- tensor_mask: int32 [16, 6], P('orb', 'grp'), parts along dimension 1, may hold values from 0 to 1, as said below
- occupied: bfloat16 [4, 2048, 384], P('grp', 'orb'), parts along dimension 0, may hold values from -0.3125 to 0.3125
- occupied_mask: int32 [4, 16, 3], P('grp', 'orb'), parts along dimension 0, may hold values from 0 to 1, as said below
- virtual: bfloat16 [4, 2048, 384], P('grp', 'orb'), parts along dimension 0, may hold values from -0.3125 to 0.3125
- virtual_mask: int32 [4, 16, 3], P('grp', 'orb'), parts along dimension 0, may hold values from 0 to 1, as said below
Outputs:
- polarizability: float32 [128, 128], P('orb', 'grp'), parts along dimension 1
The draws below stay inside these ranges and needn't reach their ends.
There are 2 independent parts, one for each index of `grp`. The reference program is written for one: setup_inputs(seed, part) draws one part's arguments, and reference() takes and returns one part's arrays. A program takes and returns all parts, laid end to end along the dimension named above; each array names one. Nothing has to cross between parts.
Inputs may be any that keep to these rules, and one draw needn't show every extreme that they name: `tensor_mask`: 0 or 1; the block on the diagonal (k = 1) is always kept, blocks outside the 16 x 16 grid are always 0; kept blocks are denser in a region of the system drawn from the seed, shared by all three patterns. `occupied_mask`: as tensor_mask. `virtual_mask`: as tensor_mask.
All inputs are finite; a program needn't handle non-finite values.
Results may differ from the reference program's by a relative error of at most 0.0041.
Values may be sent and summed in bfloat16 or wider, within the bound.
No kernel may reach another device: no remote copies, remote signals or barrier semaphores. Data moves between devices by JAX's collectives and lax.ppermute only.
A program may use at most 192 MiB of HBM per device.

```python
import jax
import jax.numpy as jnp
from jax import lax

BLK = 128
NP = 64
TIMES = 2
NB = 16
NAO = 2048


def solute_distance(key):
    centre = jax.random.randint(key, (), 0, NB)
    row_ids = jnp.arange(NB)
    distance = jnp.abs(row_ids - centre)
    return jnp.minimum(distance, NB - distance)


def screen_pattern(key, distance, lead):
    levels = jax.random.randint(key, (lead, NB, 3), 0, 16)
    threshold = jnp.where(distance < max(NB // 4, 1), 15, 4)
    retained = (levels < threshold[None, :, None]).astype(jnp.int32)
    column_ids = jnp.arange(3)[None, None, :]
    row_ids = jnp.arange(NB)[None, :, None]
    retained = jnp.where(column_ids == 1, 1, retained)
    inside = (row_ids + column_ids - 1 >= 0) & (row_ids + column_ids - 1 < NB)
    return jnp.where(inside, retained, 0).astype(jnp.int32)


def draw_tensor_mask(key, part):
    distance = solute_distance(key)
    key = jax.random.fold_in(key, 11)
    return screen_pattern(key, distance, 1)[0]


def draw_occupied_mask(key, part):
    distance = solute_distance(key)
    key = jax.random.fold_in(key, 12)
    return screen_pattern(key, distance, TIMES)


def draw_virtual_mask(key, part):
    distance = solute_distance(key)
    key = jax.random.fold_in(key, 13)
    return screen_pattern(key, distance, TIMES)


def spiked(drawn, stream_key, source, target, shards_of, factor):
    owner, partner = [(jnp.arange(drawn.shape[dim]) // (drawn.shape[dim] // shards_of)).reshape([-1 if axis == dim else 1 for axis in range(drawn.ndim)]) for dim in (source, target)]
    chosen = jax.random.permutation(stream_key, shards_of)[partner]
    strong = (owner == chosen) | (owner == (partner + shards_of // 2) % shards_of)
    return jnp.where(strong, factor * drawn, drawn)


def steps_of(stream_key, extent, shards, smallest, largest):
    gain, own = 1.0, jax.random.fold_in(stream_key, 6)
    for dim, shards_of in shards:
        heights = jnp.exp(jax.random.uniform(jax.random.fold_in(own, dim), (shards_of,), jnp.float32, smallest / len(shards), largest / len(shards)))
        gain = gain * jnp.repeat(heights, extent[dim] // shards_of).reshape([-1 if axis == dim else 1 for axis in range(len(extent))])
    return gain


def gaussian(rng, shape, scale, bound, cuts=(), kind=jnp.bfloat16):
    gain = steps_of(rng, shape, cuts, -0.22, 0.18) if cuts else 1.0
    entries = jax.random.normal(rng, shape, jnp.float32) * scale * gain
    return jnp.minimum(jnp.maximum(entries, -bound), bound).astype(kind)


def bell_draw_with(own_key, shape, scale, reach, pieces, heavy, kind=jnp.bfloat16):
    entries = scale * jax.random.normal(own_key, shape, jnp.float32)
    if pieces:
        entries = entries * steps_of(own_key, shape, pieces, -0.22, 0.18)
    return jnp.clip(spiked(entries, jax.random.fold_in(own_key, 3), *heavy), -reach, reach).astype(kind)


def setup_inputs(seed: int = 0, part: int = 0) -> dict:
    key_of = jax.random.split(jax.random.key(seed), 7)
    part_splits = jax.random.split(jax.random.fold_in(key_of[6], part), 7)
    tensor = bell_draw_with(part_splits[0], (NP, NAO, 3 * BLK), ((3 * BLK * NAO) ** -0.25), 0.25, ((1, 16),), (1, 0, 16, 2.0))
    tensor_mask = draw_tensor_mask(jax.random.fold_in(jax.random.fold_in(key_of[6], part), 71), part)
    occupied = gaussian(part_splits[2], (TIMES, NAO, 3 * BLK), (3 * BLK) ** -0.5, 0.3125, ((1, 16),))
    occupied_mask = draw_occupied_mask(jax.random.fold_in(jax.random.fold_in(key_of[6], part), 71), part)
    virtual = gaussian(part_splits[4], (TIMES, NAO, 3 * BLK), (3 * BLK) ** -0.5, 0.3125, ((1, 16),))
    virtual_mask = draw_virtual_mask(jax.random.fold_in(jax.random.fold_in(key_of[6], part), 71), part)
    return dict(tensor=tensor, tensor_mask=tensor_mask, occupied=occupied, occupied_mask=occupied_mask, virtual=virtual, virtual_mask=virtual_mask)


def screened(data, flags):
    width = data.shape[2] // 3
    shaped = data.reshape(data.shape[0], flags.shape[1], width, 3, width)
    return shaped * flags.astype(jnp.bfloat16)[:, :, None, :, None]


def reference(tensor, tensor_mask, occupied, occupied_mask, virtual, virtual_mask):
    aux_count = tensor.shape[0]
    time_count = occupied.shape[0]
    row_count = tensor_mask.shape[0]
    tens = screened(tensor, tensor_mask[None])
    occ = screened(occupied, occupied_mask)
    vir = screened(virtual, virtual_mask)
    pad_rows = ((0, 0), (1, 1), (0, 0), (0, 0), (0, 0))
    tens_pad = jnp.pad(tens, pad_rows)
    vir_pad = jnp.pad(vir, pad_rows)

    def one_row(running, row_index):
        nearby = lax.dynamic_slice_in_dim(tens_pad, row_index, 3, 1).astype(jnp.float32)
        own_rows = nearby[:, 1]
        vir_near = lax.dynamic_slice_in_dim(vir_pad, row_index, 3, 1).astype(jnp.float32)
        occ_row = lax.dynamic_index_in_dim(occ, row_index, 1, keepdims=False).astype(jnp.float32)
        results = []
        for time_idx in range(time_count):
            summed = None
            for offset in range(3):
                partial_sum = jnp.einsum('im,pmbj->pibj', occ_row[time_idx, :, offset, :], nearby[:, offset])
                widened = jnp.pad(partial_sum, ((0, 0), (0, 0), (offset, 2 - offset), (0, 0)))
                summed = widened if summed is None else summed + widened
            occupied_part = lax.optimization_barrier(summed.astype(jnp.bfloat16)).astype(jnp.float32)
            columns = [jnp.einsum('piej,sej->pis', occupied_part[:, :, shift_idx:shift_idx + 3, :], vir_near[time_idx, shift_idx]) for shift_idx in range(3)]
            virtual_part = lax.optimization_barrier(jnp.stack(columns, axis=2).astype(jnp.bfloat16)).astype(jnp.float32)
            results.append(jnp.einsum('pics,qics->pq', virtual_part, own_rows))
        return running + jnp.stack(results), None

    start = jnp.zeros((time_count, aux_count, aux_count), jnp.float32)
    running, unused = lax.scan(one_row, start, jnp.arange(row_count, dtype=jnp.int32))
    return running.reshape(time_count * aux_count, aux_count)
```

```python
import functools

import jax
import jax.numpy as jnp
from jax import lax
from jax.experimental import pallas as pl
from jax.experimental.pallas import tpu as pltpu
from jax.sharding import PartitionSpec as P

CUTS = (64, 128)
AUX_STEP = 16
GROUP = 4
ROW_STEP = 16
VMEM_LIMIT = 56 * 1024 * 1024


def dot(lhs, rhs):
    return jnp.dot(lhs, rhs, preferred_element_type=jnp.float32)


def dot_nt(lhs, rhs):
    return lax.dot_general(
        lhs, rhs, (((1,), (1,)), ((), ())), preferred_element_type=jnp.float32
    )


def flat(block):
    return pltpu.einshape("plc->p(lc)", block)


def own_kernel(
    times, width, b_ref, mask_ref, occ_ref, vir_ref, low_ref, high_ref,
    flat_ref, own_ref, wide_ref, thin_ref,
    left_w, right_w, low_w, occ_w, masked, own_n, wide_n, thin_n,
):
    w = width

    @pl.when(pl.program_id(0) == 0)
    def build():
        for t in range(times):
            v_low, v_own, v_high = (vir_ref[t, :, k * w : (k + 1) * w] for k in range(3))
            below_own, below_up = low_ref[t, :, :w], low_ref[t, :, w : 2 * w]
            above_down, above_own = high_ref[t, :, :w], high_ref[t, :, w : 2 * w]

            def cols(slot):
                return slice((slot * times + t) * w, (slot * times + t + 1) * w)

            left_w[:, cols(0)] = v_low.T
            left_w[:, cols(1)] = below_up
            right_w[:w, cols(0)] = v_own.T
            right_w[w:, cols(0)] = v_high.T
            right_w[:w, cols(1)] = v_own
            right_w[w:, cols(1)] = above_down
            right_w[:w, cols(2)] = above_down.T
            right_w[w:, cols(2)] = above_own.T
            low_w[:w, cols(0)] = below_own.T
            low_w[w:, cols(0)] = below_up.T
            low_w[:w, cols(1)] = below_own
            low_w[w:, cols(1)] = v_low

            occ_w[t, 0] = occ_ref[t, :, w : 2 * w]
            occ_w[t, 1] = low_ref[t, :, 2 * w :]
            occ_w[t, 2] = occ_ref[t, :, :w].T
            occ_w[t, 3] = high_ref[t, :, 2 * w :]
            occ_w[t, 4] = occ_ref[t, :, 2 * w :].T

    masked[...] = b_ref[...] * mask_ref[...]
    flat_ref[...] = flat(masked[...])

    def group(g, carry):
        first = g * GROUP
        rows = masked[pl.ds(first, GROUP)].reshape(GROUP * w, 3 * w)
        from_left = dot(rows[:, :w], left_w[...])
        from_right = dot(rows[:, w:], right_w[...])
        from_low = dot(rows[:, : 2 * w], low_w[...])

        def part(product, slot, t):
            return product[:, (slot * times + t) * w : (slot * times + t + 1) * w]

        for t in range(times):
            left_c, left_b = part(from_left, 0, t), part(from_left, 1, t)
            u_low = part(from_low, 0, t).astype(jnp.bfloat16)
            u_mid = (part(from_right, 0, t) + left_c).astype(jnp.bfloat16)
            u_top = part(from_right, 2, t).astype(jnp.bfloat16)
            x_low = part(from_low, 1, t).astype(jnp.bfloat16)
            x_mid = (part(from_right, 1, t) + left_b).astype(jnp.bfloat16)
            left_c, left_b = left_c.astype(jnp.bfloat16), left_b.astype(jnp.bfloat16)
            o_both = occ_w[t, 0:2].reshape(2 * w, w)
            for j in range(GROUP):
                p = first + j
                r = slice(j * w, (j + 1) * w)
                both = dot(o_both, jnp.concatenate([u_low[r], u_mid[r]], axis=1))
                both = both.astype(jnp.bfloat16)
                own_n[t, p, :, : 2 * w] = both[:w]
                wide_n[t, p] = both[w:]
                own_n[t, p, :, 2 * w :] = dot(occ_w[t, 0], u_top[r]).astype(jnp.bfloat16)
                wide_n[times + t, p] = dot(
                    occ_w[t, 2], jnp.concatenate([x_low[r], x_mid[r]], axis=1)
                ).astype(jnp.bfloat16)
                thin_n[t, p] = dot(occ_w[t, 3], left_c[r]).astype(jnp.bfloat16)
                thin_n[times + t, p] = dot(occ_w[t, 4], left_b[r]).astype(jnp.bfloat16)
        return carry

    lax.fori_loop(0, AUX_STEP // GROUP, group, 0)
    for t in range(times):
        own_ref[t] = flat(own_n[t])
    for s in range(2 * times):
        wide_ref[s] = flat(wide_n[s])
        thin_ref[s] = flat(thin_n[s])


def own_terms(tensor, mask_row, occ, vir, low, high):
    aux, w, band = tensor.shape
    times = occ.shape[0]
    bf = jnp.bfloat16
    whole = pl.BlockSpec((times, w, band), lambda i: (0, 0, 0))
    flops = 2 * aux * w * w * w * (14 * times + 9 * times)
    return pl.pallas_call(
        functools.partial(own_kernel, times, w),
        grid=(aux // AUX_STEP,),
        in_specs=[
            pl.BlockSpec((AUX_STEP, w, band), lambda i: (i, 0, 0)),
            pl.BlockSpec((1, 1, band), lambda i: (0, 0, 0)),
            whole, whole, whole, whole,
        ],
        out_specs=[
            pl.BlockSpec((AUX_STEP, w * band), lambda i: (i, 0)),
            pl.BlockSpec((times, AUX_STEP, w * band), lambda i: (0, i, 0)),
            pl.BlockSpec((2 * times, AUX_STEP, 2 * w * w), lambda i: (0, i, 0)),
            pl.BlockSpec((2 * times, AUX_STEP, w * w), lambda i: (0, i, 0)),
        ],
        out_shape=[
            jax.ShapeDtypeStruct((aux, w * band), bf),
            jax.ShapeDtypeStruct((times, aux, w * band), bf),
            jax.ShapeDtypeStruct((2 * times, aux, 2 * w * w), bf),
            jax.ShapeDtypeStruct((2 * times, aux, w * w), bf),
        ],
        scratch_shapes=[
            pltpu.VMEM((w, 2 * times * w), bf),
            pltpu.VMEM((2 * w, 3 * times * w), bf),
            pltpu.VMEM((2 * w, 2 * times * w), bf),
            pltpu.VMEM((times, 5, w, w), bf),
            pltpu.VMEM((AUX_STEP, w, band), bf),
            pltpu.VMEM((times, AUX_STEP, w, band), bf),
            pltpu.VMEM((2 * times, AUX_STEP, w, 2 * w), bf),
            pltpu.VMEM((2 * times, AUX_STEP, w, w), bf),
        ],
        compiler_params=pltpu.CompilerParams(vmem_limit_bytes=VMEM_LIMIT),
        cost_estimate=pl.CostEstimate(flops=flops, bytes_accessed=50_000_000, transcendentals=0),
        name="own_terms",
    )(tensor, mask_row, occ, vir, low, high)


def own_sum_kernel(times, aux, own_ref, flat_ref, out_ref):
    @pl.when(pl.program_id(0) == 0)
    def start():
        out_ref[...] = jnp.zeros_like(out_ref)

    out_ref[: times * aux] += dot_nt(
        own_ref[...].reshape(times * aux, own_ref.shape[2]), flat_ref[...]
    )


def own_sum(own, flat_rows):
    times, aux, length = own.shape
    step = length // 8
    return pl.pallas_call(
        functools.partial(own_sum_kernel, times, aux),
        grid=(8,),
        in_specs=[
            pl.BlockSpec((times, aux, step), lambda i: (0, 0, i)),
            pl.BlockSpec((aux, step), lambda i: (0, i)),
        ],
        out_specs=pl.BlockSpec((2 * times * aux, aux), lambda i: (0, 0)),
        out_shape=jax.ShapeDtypeStruct((2 * times * aux, aux), jnp.float32),
        compiler_params=pltpu.CompilerParams(vmem_limit_bytes=VMEM_LIMIT),
        cost_estimate=pl.CostEstimate(
            flops=2 * times * aux * aux * length, bytes_accessed=20_000_000, transcendentals=0
        ),
        name="own_sum",
    )(own, flat_rows)


def near_sum_kernel(last, times, aux, acc_ref, wide_ref, thin_ref, x_ref, l_ref, out_ref, total):
    step = pl.program_id(0)

    @pl.when(step == 0)
    def start():
        total[...] = acc_ref[...]

    slots = 2 * times * aux
    total[...] += dot_nt(wide_ref[...].reshape(slots, wide_ref.shape[2]), flat(x_ref[...])) + dot_nt(
        thin_ref[...].reshape(slots, thin_ref.shape[2]), flat(l_ref[...])
    )

    @pl.when(step == pl.num_programs(0) - 1)
    def finish():
        if last:
            for t in range(times):
                swapped = total[(times + t) * aux : (times + t + 1) * aux].T
                out_ref[t * aux : (t + 1) * aux] = total[t * aux : (t + 1) * aux] + swapped
        else:
            out_ref[...] = total[...]


def near_sum(acc, wide, thin, x, l, first_row, last):
    slots, aux, _ = wide.shape
    times = slots // 2
    rows, w = x.shape[1], l.shape[2]
    base = first_row // ROW_STEP
    out_rows = times * aux if last else slots * aux
    return pl.pallas_call(
        functools.partial(near_sum_kernel, last, times, aux),
        grid=(rows // ROW_STEP,),
        in_specs=[
            pl.BlockSpec((slots * aux, aux), lambda i: (0, 0)),
            pl.BlockSpec((slots, aux, ROW_STEP * 2 * w), lambda i: (0, 0, base + i)),
            pl.BlockSpec((slots, aux, ROW_STEP * w), lambda i: (0, 0, base + i)),
            pl.BlockSpec((aux, ROW_STEP, 2 * w), lambda i: (0, i, 0)),
            pl.BlockSpec((aux, ROW_STEP, w), lambda i: (0, i, 0)),
        ],
        out_specs=pl.BlockSpec((out_rows, aux), lambda i: (0, 0)),
        out_shape=jax.ShapeDtypeStruct((out_rows, aux), jnp.float32),
        scratch_shapes=[pltpu.VMEM((slots * aux, aux), jnp.float32)],
        compiler_params=pltpu.CompilerParams(vmem_limit_bytes=VMEM_LIMIT),
        cost_estimate=pl.CostEstimate(
            flops=2 * slots * aux * aux * rows * 3 * w,
            bytes_accessed=2 * (slots + 1) * aux * rows * 3 * w,
            transcendentals=0,
        ),
        name="near_sum",
    )(acc, wide, thin, x, l)


def scattered_sum(value, axis):
    count = lax.axis_size(axis)
    me = lax.axis_index(axis)
    share = value.shape[0] // count
    if count & (count - 1):
        return lax.dynamic_slice_in_dim(lax.psum(value, axis), me * share, share, 0)
    bits = count.bit_length() - 1
    current = value.reshape((2,) * bits + (share, value.shape[1]))
    for bit in range(bits):
        dim = bits - 1 - bit
        mine = (me >> bit) & 1
        keep = lax.dynamic_index_in_dim(current, mine, dim, keepdims=False)
        send = lax.dynamic_index_in_dim(current, 1 - mine, dim, keepdims=False)
        pairs = [(i, i ^ (1 << bit)) for i in range(count)]
        current = keep + lax.ppermute(send, axis, pairs)
    return current


def body(tensor, tensor_mask, occupied, occupied_mask, virtual, virtual_mask):
    w = tensor.shape[1]
    bf = jnp.bfloat16
    count = lax.axis_size("orb")
    forward = [(i, i + 1) for i in range(count - 1)]
    backward = [(i + 1, i) for i in range(count - 1)]

    def spread(flags):
        return jnp.repeat(flags.astype(bf), w, axis=-1)

    mask_row = spread(tensor_mask)[:, None, :]
    occ = occupied * spread(occupied_mask)
    vir = virtual * spread(virtual_mask)
    low = lax.ppermute(jnp.concatenate([vir[:, :, w:], occ[:, :, 2 * w :]], 2), "orb", forward)
    high = lax.ppermute(jnp.concatenate([vir[:, :, : 2 * w], occ[:, :, :w]], 2), "orb", backward)

    arrived = []
    begin = 0
    for end in CUTS:
        x = tensor[:, begin:end, w:] * mask_row[:, :, w:]
        l = tensor[:, begin:end, :w] * mask_row[:, :, :w]
        arrived.append((begin, lax.ppermute(x, "orb", forward), lax.ppermute(l, "orb", backward)))
        begin = end

    flat_rows, own, wide, thin = own_terms(tensor, mask_row, occ, vir, low, high)
    total = own_sum(own, flat_rows)
    for index, (begin, x, l) in enumerate(arrived):
        total = near_sum(total, wide, thin, x, l, begin, index == len(arrived) - 1)
    return scattered_sum(total, "orb")


def solution(mesh):
    return jax.shard_map(
        body,
        mesh=mesh,
        in_specs=(
            P("grp", "orb", None),
            P("orb", "grp"),
            P("grp", "orb", None),
            P("grp", "orb", None),
            P("grp", "orb", None),
            P("grp", "orb", None),
        ),
        out_specs=P("orb", "grp"),
        check_vma=False,
    )
```

```python
import functools

import jax
import jax.numpy as jnp
from jax import lax
from jax.experimental import pallas as pl
from jax.experimental.pallas import tpu as pltpu
from jax.sharding import PartitionSpec as P

CUTS = ((96, 32), (0, 80), (80, 16))
AUX_STEP = 16
GROUP = 4
ROW_STEP = 16
VMEM_LIMIT = 60 * 1024 * 1024
HBM = pl.BlockSpec(memory_space=pltpu.HBM)
SMEM = pl.BlockSpec(memory_space=pltpu.SMEM)


def dot(lhs, rhs):
    return jnp.dot(lhs, rhs, preferred_element_type=jnp.float32)


def dot_nt(lhs, rhs):
    return lax.dot_general(
        lhs, rhs, (((1,), (1,)), ((), ())), preferred_element_type=jnp.float32
    )


def flat(block):
    return pltpu.einshape("plc->p(lc)", block)


def kept(flag, block):
    return jnp.where(flag != 0, block, jnp.zeros_like(block))


def part(ref, t, k, width, flag):
    return kept(flag[t, 0, k], ref[t, :, k * width : (k + 1) * width])


def cut_blocks(width, b_ref, flag_ref, x_ref, l_ref):
    w = width
    l_ref[...] = kept(flag_ref[0, 0], b_ref[:, :, :w])
    x_ref[:, :, :w] = kept(flag_ref[0, 1], b_ref[:, :, w : 2 * w])
    x_ref[:, :, w:] = kept(flag_ref[0, 2], b_ref[:, :, 2 * w :])


def first_cut_kernel(
    times, width, rows, b_ref, flag_ref, occ_ref, vir_ref, occ_flag, vir_flag, x_ref, l_ref
):
    w, pieces = width, width // rows
    occ = functools.partial(part, occ_ref, width=w, flag=occ_flag)
    vir = functools.partial(part, vir_ref, width=w, flag=vir_flag)
    sent_up = [(vir(t, 1), vir(t, 2)) for t in range(times)]
    flat_occ = [occ(t, 2) for t in range(times)]
    sent_up += list(zip(flat_occ[::2], flat_occ[1::2], strict=True))
    for n, (one, two) in enumerate(sent_up):
        where = slice(n * pieces, (n + 1) * pieces)
        x_ref[where, :, :w] = one.reshape(pieces, rows, w)
        x_ref[where, :, w:] = two.reshape(pieces, rows, w)
    sent_down = [f(t, k) for t in range(times) for f, k in ((vir, 0), (vir, 1), (occ, 0))]
    for n, one in enumerate(sent_down):
        l_ref[n * pieces : (n + 1) * pieces] = one.reshape(pieces, rows, w)
    x_head, l_head = heads(times, w, rows)
    cut_blocks(w, b_ref, flag_ref, x_ref.at[x_head:], l_ref.at[l_head:])


def heads(times, width, rows):
    pieces = width // rows
    return 3 * times // 2 * pieces, 3 * times * pieces


def first_cut(tensor, flag, occ, vir, occ_flag, vir_flag):
    aux, w, band = tensor.shape
    times = occ.shape[0]
    begin, rows = CUTS[0]
    x_head, l_head = heads(times, w, rows)
    whole = pl.BlockSpec(occ.shape, lambda i: (0, 0, 0))
    x_shape, l_shape = (x_head + aux, rows, 2 * w), (l_head + aux, rows, w)
    return pl.pallas_call(
        functools.partial(first_cut_kernel, times, w, rows),
        grid=(1,),
        in_specs=[
            pl.BlockSpec((aux, rows, band), lambda i: (0, begin // rows, 0)),
            SMEM, whole, whole, SMEM, SMEM,
        ],
        out_specs=[pl.BlockSpec(n, lambda i: (0, 0, 0)) for n in (x_shape, l_shape)],
        out_shape=[jax.ShapeDtypeStruct(n, tensor.dtype) for n in (x_shape, l_shape)],
        compiler_params=pltpu.CompilerParams(vmem_limit_bytes=VMEM_LIMIT),
        name="first_cut",
    )(tensor, flag, occ, vir, occ_flag, vir_flag)


def later_cut(tensor, flag, begin, rows):
    aux, w, band = tensor.shape
    return pl.pallas_call(
        functools.partial(cut_blocks, w),
        grid=(aux // AUX_STEP,),
        in_specs=[pl.BlockSpec((AUX_STEP, rows, band), lambda i: (i, begin // rows, 0)), SMEM],
        out_specs=[
            pl.BlockSpec((AUX_STEP, rows, 2 * w), lambda i: (i, 0, 0)),
            pl.BlockSpec((AUX_STEP, rows, w), lambda i: (i, 0, 0)),
        ],
        out_shape=[
            jax.ShapeDtypeStruct((aux, rows, 2 * w), tensor.dtype),
            jax.ShapeDtypeStruct((aux, rows, w), tensor.dtype),
        ],
        compiler_params=pltpu.CompilerParams(vmem_limit_bytes=VMEM_LIMIT),
        name="later_cut",
    )(tensor, flag)


def own_kernel(
    times, width, b_ref, flag_ref, occ_ref, vir_ref, occ_flag, vir_flag, up_ref, down_ref,
    sum_ref, wide_ref, thin_ref,
    left_w, right_w, low_w, occ_w, masked, u, x, left, own_n, wide_n, thin_n, flat_own, flat_b,
):
    w = width
    step = pl.program_id(0)

    @pl.when(step == 0)
    def build():
        pieces = w // up_ref.shape[1]

        def got(ref, n, lanes=slice(None)):
            return ref[n * pieces : (n + 1) * pieces, :, lanes].reshape(w, w)

        one, two = slice(None, w), slice(w, None)
        for t in range(times):
            v_low, v_own, v_high = (part(vir_ref, t, k, w, vir_flag) for k in range(3))
            o_low, o_own, o_high = (part(occ_ref, t, k, w, occ_flag) for k in range(3))
            below_own, below_up = got(up_ref, t, one), got(up_ref, t, two)
            below_occ = got(up_ref, times + t // 2, (one, two)[t % 2])
            above_down, above_own, above_occ = (got(down_ref, 3 * t + n) for n in range(3))

            def cols(slot):
                return slice((slot * times + t) * w, (slot * times + t + 1) * w)

            left_w[:, cols(0)] = v_low.T
            left_w[:, cols(1)] = below_up
            right_w[:w, cols(0)] = v_own.T
            right_w[w:, cols(0)] = v_high.T
            right_w[:w, cols(1)] = v_own
            right_w[w:, cols(1)] = above_down
            right_w[:w, cols(2)] = above_down.T
            right_w[w:, cols(2)] = above_own.T
            low_w[:w, cols(0)] = below_own.T
            low_w[w:, cols(0)] = below_up.T
            low_w[:w, cols(1)] = below_own
            low_w[w:, cols(1)] = v_low

            occ_w[t, 0] = o_own
            occ_w[t, 1] = below_occ
            occ_w[t, 2] = o_low.T
            occ_w[t, 3] = above_occ
            occ_w[t, 4] = o_high.T

    bf = jnp.bfloat16
    for k in range(3):
        block = slice(k * w, (k + 1) * w)
        masked[:, :, block] = kept(flag_ref[0, k], b_ref[:, :, block])

    loops = AUX_STEP // GROUP
    rows = w // loops
    here = pl.ds(pl.multiple_of(step * AUX_STEP, AUX_STEP), AUX_STEP)

    def lay(g, source, target):
        first = pl.multiple_of(g * rows, rows)
        length = rows * source.shape[2]
        at = pl.ds(pl.multiple_of(g * length, length), length)
        target(at, flat(source[:, pl.ds(first, rows), :]))

    def to_own(t):
        def store(at, value):
            flat_own[t, here, at] = value

        return store

    def to_b(at, value):
        flat_b[here, at] = value

    def to_out(ref, slot):
        def store(at, value):
            ref[slot, :, at] = value

        return store

    def virtual_phase(g):
        group = pl.ds(g * GROUP, GROUP)
        lhs = masked[group].reshape(GROUP * w, 3 * w)
        from_left = dot(lhs[:, :w], left_w[...])
        from_right = dot(lhs[:, w:], right_w[...])
        from_low = dot(lhs[:, : 2 * w], low_w[...])

        def piece(product, slot, t):
            return product[:, (slot * times + t) * w : (slot * times + t + 1) * w]

        def put(ref, t, lanes, value):
            ref[t, group, :, lanes] = value.astype(bf).reshape(GROUP, w, w)

        one, two, three = slice(None, w), slice(w, 2 * w), slice(2 * w, None)
        for t in range(times):
            left_c, left_b = piece(from_left, 0, t), piece(from_left, 1, t)
            put(u, t, one, piece(from_low, 0, t))
            put(u, t, two, piece(from_right, 0, t) + left_c)
            put(u, t, three, piece(from_right, 2, t))
            put(x, t, one, piece(from_low, 1, t))
            put(x, t, two, piece(from_right, 1, t) + left_b)
            put(left, t, one, left_c)
            put(left, t, two, left_b)

    def pairs(g):
        return [(g * GROUP + j, g * GROUP + j + 1) for j in range(0, GROUP, 2)]

    def in_pair(occ, source, lanes, target, lanes_to, p, q):
        both = dot(occ, jnp.concatenate([source[p, :, lanes], source[q, :, lanes]], axis=1))
        both = both.astype(bf)
        target[p, :, lanes_to] = both[:, :w]
        target[q, :, lanes_to] = both[:, w:]

    def own_phase(t, g):
        occ = occ_w[t, 0:2].reshape(2 * w, w)
        for j in range(GROUP):
            p = g * GROUP + j
            both = dot(occ, u[t, p, :, : 2 * w]).astype(bf)
            own_n[t, p, :, : 2 * w] = both[:w]
            wide_n[t, p] = both[w:]
        last = slice(2 * w, 3 * w)
        for p, q in pairs(g):
            in_pair(occ_w[t, 0], u.at[t], last, own_n.at[t], last, p, q)

    def other_phase(t, g):
        for j in range(GROUP):
            p = g * GROUP + j
            wide_n[times + t, p] = dot(occ_w[t, 2], x[t, p]).astype(bf)
        for p, q in pairs(g):
            every = slice(None)
            in_pair(occ_w[t, 3], left.at[t], slice(None, w), thin_n.at[t], every, p, q)
            in_pair(occ_w[t, 4], left.at[t], slice(w, None), thin_n.at[times + t], every, p, q)

    def lay_b(g):
        lay(g, masked, to_b)

    def lay_own(t, g):
        lay(g, own_n.at[t], to_own(t))
        lay(g, wide_n.at[t], to_out(wide_ref, t))

    def lay_other(t, g):
        lay(g, wide_n.at[times + t], to_out(wide_ref, times + t))
        lay(g, thin_n.at[t], to_out(thin_ref, t))
        lay(g, thin_n.at[times + t], to_out(thin_ref, times + t))

    work, laying = [virtual_phase], [lay_b]
    for t in range(times):
        work += [functools.partial(own_phase, t), functools.partial(other_phase, t)]
        laying += [functools.partial(lay_own, t), functools.partial(lay_other, t)]
    for n, phase in enumerate(work):

        def both(g, carry, phase=phase, before=laying[n - 1] if n else None):
            phase(g)
            if before is not None:
                before(g)
            return carry

        lax.fori_loop(0, loops, both, 0)
    for g in range(loops):
        laying[-1](g)

    @pl.when(step == pl.num_programs(0) - 1)
    def add_up():
        count = times * flat_own.shape[1]
        length = flat_own.shape[2]
        share = length // 8
        total = None
        for n in range(8):
            at = slice(n * share, (n + 1) * share)
            term = dot_nt(flat_own[:, :, at].reshape(count, share), flat_b[:, at])
            total = term if total is None else total + term
        sum_ref[...] = total


def own_terms(tensor, flag, occ, vir, occ_flag, vir_flag, up, down):
    aux, w, band = tensor.shape
    times = occ.shape[0]
    bf = jnp.bfloat16
    x_head, l_head = heads(times, w, CUTS[0][1])

    def whole(shape):
        return pl.BlockSpec(shape, lambda i: (0, 0, 0))

    flops = 2 * aux * w * w * w * (14 * times + 9 * times)
    return pl.pallas_call(
        functools.partial(own_kernel, times, w),
        grid=(aux // AUX_STEP,),
        in_specs=[
            pl.BlockSpec((AUX_STEP, w, band), lambda i: (i, 0, 0)),
            SMEM, whole(occ.shape), whole(vir.shape), SMEM, SMEM,
            whole((x_head, *up.shape[1:])), whole((l_head, *down.shape[1:])),
        ],
        out_specs=[
            pl.BlockSpec((times * aux, aux), lambda i: (0, 0)),
            pl.BlockSpec((2 * times, AUX_STEP, 2 * w * w), lambda i: (0, i, 0)),
            pl.BlockSpec((2 * times, AUX_STEP, w * w), lambda i: (0, i, 0)),
        ],
        out_shape=[
            jax.ShapeDtypeStruct((times * aux, aux), jnp.float32),
            jax.ShapeDtypeStruct((2 * times, aux, 2 * w * w), bf),
            jax.ShapeDtypeStruct((2 * times, aux, w * w), bf),
        ],
        scratch_shapes=[
            pltpu.VMEM((w, 2 * times * w), bf),
            pltpu.VMEM((2 * w, 3 * times * w), bf),
            pltpu.VMEM((2 * w, 2 * times * w), bf),
            pltpu.VMEM((times, 5, w, w), bf),
            pltpu.VMEM((AUX_STEP, w, band), bf),
            pltpu.VMEM((times, AUX_STEP, w, band), bf),
            pltpu.VMEM((times, AUX_STEP, w, 2 * w), bf),
            pltpu.VMEM((times, AUX_STEP, w, 2 * w), bf),
            pltpu.VMEM((times, AUX_STEP, w, band), bf),
            pltpu.VMEM((2 * times, AUX_STEP, w, 2 * w), bf),
            pltpu.VMEM((2 * times, AUX_STEP, w, w), bf),
            pltpu.VMEM((times, aux, w * band), bf),
            pltpu.VMEM((aux, w * band), bf),
        ],
        compiler_params=pltpu.CompilerParams(vmem_limit_bytes=VMEM_LIMIT),
        cost_estimate=pl.CostEstimate(flops=flops, bytes_accessed=50_000_000, transcendentals=0),
        name="own_terms",
    )(tensor, flag, occ, vir, occ_flag, vir_flag, up, down)


def near_kernel(begin, steps, skips, earlier, wide_hbm, thin_hbm, x_hbm, l_hbm, *rest):
    before, rest = rest[:earlier], rest[earlier:]
    out_ref, wide, thin, x, l, held, sems, held_sems = rest
    slots, aux, w = wide.shape[1], wide.shape[2], l.shape[3]
    times = slots // 2

    def copies(s):
        rows = pl.ds(s * ROW_STEP, ROW_STEP)
        far = begin + s * ROW_STEP
        return [
            pltpu.make_async_copy(
                wide_hbm.at[:, :, pl.ds(far * 2 * w, ROW_STEP * 2 * w)], wide.at[s], sems.at[s, 0]
            ),
            pltpu.make_async_copy(
                thin_hbm.at[:, :, pl.ds(far * w, ROW_STEP * w)], thin.at[s], sems.at[s, 1]
            ),
            pltpu.make_async_copy(x_hbm.at[pl.ds(skips[0], aux), rows], x.at[s], sems.at[s, 2]),
            pltpu.make_async_copy(l_hbm.at[pl.ds(skips[1], aux), rows], l.at[s], sems.at[s, 3]),
        ]

    fetch = []
    for n, ref in enumerate(before):
        size = ref.shape[0]
        fetch.append(
            pltpu.make_async_copy(ref, held.at[n, pl.ds(0, size)], held_sems.at[n])
        )
    for s in range(steps):
        for copy in copies(s):
            copy.start()
    for copy in fetch:
        copy.start()
    total = None
    for s in range(steps):
        for copy in copies(s):
            copy.wait()
        wide_s = wide[s].reshape(slots * aux, ROW_STEP * 2 * w)
        thin_s = thin[s].reshape(slots * aux, ROW_STEP * w)
        term = dot_nt(wide_s, flat(x[s])) + dot_nt(thin_s, flat(l[s]))
        total = term if total is None else total + term
    if not earlier:
        out_ref[...] = total
        return
    for copy in fetch:
        copy.wait()
    half = times * aux
    for n in range(1, earlier):
        total = total + held[n]
    for t in range(times):
        rows = slice(t * aux, (t + 1) * aux)
        out_ref[rows] = held[0, rows] + total[rows] + total[half + t * aux : half + (t + 1) * aux].T


def near_sum(wide, thin, x, l, begin, rows, before=()):
    slots, aux, _ = wide.shape
    w = l.shape[2]
    steps = rows // ROW_STEP
    skips = (x.shape[0] - aux, l.shape[0] - aux)
    shape = (slots // 2 * aux if before else slots * aux, aux)
    bf = jnp.bfloat16
    return pl.pallas_call(
        functools.partial(near_kernel, begin, steps, skips, len(before)),
        in_specs=[HBM] * (4 + len(before)),
        out_specs=pl.BlockSpec(memory_space=pltpu.VMEM),
        out_shape=jax.ShapeDtypeStruct(shape, jnp.float32),
        scratch_shapes=[
            pltpu.VMEM((steps, slots, aux, ROW_STEP * 2 * w), bf),
            pltpu.VMEM((steps, slots, aux, ROW_STEP * w), bf),
            pltpu.VMEM((steps, aux, ROW_STEP, 2 * w), bf),
            pltpu.VMEM((steps, aux, ROW_STEP, w), bf),
            pltpu.VMEM((max(len(before), 1), slots * aux, aux), jnp.float32),
            pltpu.SemaphoreType.DMA((steps, 4)),
            pltpu.SemaphoreType.DMA((max(len(before), 1),)),
        ],
        compiler_params=pltpu.CompilerParams(vmem_limit_bytes=VMEM_LIMIT),
        cost_estimate=pl.CostEstimate(
            flops=2 * slots * aux * aux * rows * 3 * w,
            bytes_accessed=2 * (slots + 1) * aux * rows * 3 * w,
            transcendentals=0,
        ),
        name="near_sum",
    )(wide, thin, x, l, *before)


def scattered_sum(value, axis):
    count = lax.axis_size(axis)
    me = lax.axis_index(axis)
    share = value.shape[0] // count
    if count & (count - 1):
        return lax.dynamic_slice_in_dim(lax.psum(value, axis), me * share, share, 0)
    bits = count.bit_length() - 1
    current = value.reshape((2,) * bits + (share, value.shape[1]))
    left = list(range(bits))
    while left:
        chosen = left[-2:]

        def pick(flips):
            block = current
            for bit in chosen:
                dim = len(left) - 1 - left.index(bit)
                at = ((me >> bit) & 1) ^ ((flips >> bit) & 1)
                block = lax.dynamic_slice_in_dim(block, at, 1, dim)
            return block.reshape((2,) * (len(left) - len(chosen)) + (share, value.shape[1]))

        total = pick(0)
        for code in range(1, 1 << len(chosen)):
            flips = sum(((code >> j) & 1) << bit for j, bit in enumerate(chosen))
            pairs = [(i, i ^ flips) for i in range(count)]
            total = total + lax.ppermute(pick(flips), axis, pairs)
        current = total
        left = left[: len(left) - len(chosen)]
    return current


def body(tensor, tensor_mask, occupied, occupied_mask, virtual, virtual_mask):
    count = lax.axis_size("orb")
    forward = [(i, i + 1) for i in range(count - 1)]
    backward = [(i + 1, i) for i in range(count - 1)]

    arrived = []
    source = tensor
    for begin, rows in CUTS:
        if not arrived:
            x, l = first_cut(
                tensor, tensor_mask, occupied, virtual, occupied_mask, virtual_mask
            )
        else:
            x, l = later_cut(source, tensor_mask, begin, rows)
        source, x, l = lax.optimization_barrier((source, x, l))
        arrived.append((lax.ppermute(x, "orb", forward), lax.ppermute(l, "orb", backward)))

    total, wide, thin = own_terms(
        tensor, tensor_mask, occupied, virtual, occupied_mask, virtual_mask, *arrived[0]
    )
    before = [total]
    for (begin, rows), (x, l) in zip(CUTS, arrived, strict=True):
        last = len(before) == len(CUTS)
        before.append(near_sum(wide, thin, x, l, begin, rows, before if last else ()))
    return scattered_sum(before[-1], "orb")


def solution(mesh):
    return jax.shard_map(
        body,
        mesh=mesh,
        in_specs=(
            P("grp", "orb", None),
            P("orb", "grp"),
            P("grp", "orb", None),
            P("grp", "orb", None),
            P("grp", "orb", None),
            P("grp", "orb", None),
        ),
        out_specs=P("orb", "grp"),
        check_vma=False,
    )
```

```python
import functools

import jax
import jax.numpy as jnp
from jax import lax
from jax.experimental import pallas as pl
from jax.experimental.pallas import tpu as pltpu
from jax.sharding import PartitionSpec as P

CUTS = ((112, 16), (0, 96), (96, 16))
AUX_STEP = 16
GROUP = 4
ROW_STEP = 16
VMEM_LIMIT = 60 * 1024 * 1024
HBM = pl.BlockSpec(memory_space=pltpu.HBM)
SMEM = pl.BlockSpec(memory_space=pltpu.SMEM)


def dot(lhs, rhs):
    return jnp.dot(lhs, rhs, preferred_element_type=jnp.float32)


def dot_nt(lhs, rhs):
    return lax.dot_general(
        lhs, rhs, (((1,), (1,)), ((), ())), preferred_element_type=jnp.float32
    )


def flat(block):
    return pltpu.einshape("plc->p(lc)", block)


def kept(flag, block):
    return jnp.where(flag != 0, block, jnp.zeros_like(block))


def part(ref, t, k, width, flag):
    return kept(flag[t, 0, k], ref[t, :, k * width : (k + 1) * width])


def cut_blocks(width, b_ref, flag_ref, x_ref, l_ref):
    w = width
    l_ref[...] = kept(flag_ref[0, 0], b_ref[:, :, :w])
    x_ref[:, :, :w] = kept(flag_ref[0, 1], b_ref[:, :, w : 2 * w])
    x_ref[:, :, w:] = kept(flag_ref[0, 2], b_ref[:, :, 2 * w :])


def first_cut_kernel(
    times, width, rows, b_ref, flag_ref, occ_ref, vir_ref, occ_flag, vir_flag, x_ref, l_ref
):
    w, pieces = width, width // rows
    occ = functools.partial(part, occ_ref, width=w, flag=occ_flag)
    vir = functools.partial(part, vir_ref, width=w, flag=vir_flag)
    sent_up = [(vir(t, 1), vir(t, 2)) for t in range(times)]
    flat_occ = [occ(t, 2) for t in range(times)]
    sent_up += list(zip(flat_occ[::2], flat_occ[1::2], strict=True))
    for n, (one, two) in enumerate(sent_up):
        where = slice(n * pieces, (n + 1) * pieces)
        x_ref[where, :, :w] = one.reshape(pieces, rows, w)
        x_ref[where, :, w:] = two.reshape(pieces, rows, w)
    sent_down = [f(t, k) for t in range(times) for f, k in ((vir, 0), (vir, 1), (occ, 0))]
    for n, one in enumerate(sent_down):
        l_ref[n * pieces : (n + 1) * pieces] = one.reshape(pieces, rows, w)
    x_head, l_head = heads(times, w, rows)
    cut_blocks(w, b_ref, flag_ref, x_ref.at[x_head:], l_ref.at[l_head:])


def heads(times, width, rows):
    pieces = width // rows
    return 3 * times // 2 * pieces, 3 * times * pieces


def first_cut(tensor, flag, occ, vir, occ_flag, vir_flag):
    aux, w, band = tensor.shape
    times = occ.shape[0]
    begin, rows = CUTS[0]
    x_head, l_head = heads(times, w, rows)
    whole = pl.BlockSpec(occ.shape, lambda i: (0, 0, 0))
    x_shape, l_shape = (x_head + aux, rows, 2 * w), (l_head + aux, rows, w)
    return pl.pallas_call(
        functools.partial(first_cut_kernel, times, w, rows),
        grid=(1,),
        in_specs=[
            pl.BlockSpec((aux, rows, band), lambda i: (0, begin // rows, 0)),
            SMEM, whole, whole, SMEM, SMEM,
        ],
        out_specs=[pl.BlockSpec(n, lambda i: (0, 0, 0)) for n in (x_shape, l_shape)],
        out_shape=[jax.ShapeDtypeStruct(n, tensor.dtype) for n in (x_shape, l_shape)],
        compiler_params=pltpu.CompilerParams(vmem_limit_bytes=VMEM_LIMIT),
        name="first_cut",
    )(tensor, flag, occ, vir, occ_flag, vir_flag)


def later_cut(tensor, flag, begin, rows):
    aux, w, band = tensor.shape
    return pl.pallas_call(
        functools.partial(cut_blocks, w),
        grid=(aux // AUX_STEP,),
        in_specs=[pl.BlockSpec((AUX_STEP, rows, band), lambda i: (i, begin // rows, 0)), SMEM],
        out_specs=[
            pl.BlockSpec((AUX_STEP, rows, 2 * w), lambda i: (i, 0, 0)),
            pl.BlockSpec((AUX_STEP, rows, w), lambda i: (i, 0, 0)),
        ],
        out_shape=[
            jax.ShapeDtypeStruct((aux, rows, 2 * w), tensor.dtype),
            jax.ShapeDtypeStruct((aux, rows, w), tensor.dtype),
        ],
        compiler_params=pltpu.CompilerParams(vmem_limit_bytes=VMEM_LIMIT),
        name="later_cut",
    )(tensor, flag)


def own_kernel(
    times, width, b_ref, flag_ref, occ_ref, vir_ref, occ_flag, vir_flag, up_ref, down_ref,
    sum_ref, wide_ref, thin_ref,
    left_w, right_w, low_w, occ_w, masked, u, x, left, own_n, wide_n, thin_n, flat_own, flat_b,
):
    w = width
    step = pl.program_id(0)

    @pl.when(step == 0)
    def build():
        pieces = w // up_ref.shape[1]

        def got(ref, n, lanes=slice(None)):
            return ref[n * pieces : (n + 1) * pieces, :, lanes].reshape(w, w)

        one, two = slice(None, w), slice(w, None)
        for t in range(times):
            v_low, v_own, v_high = (part(vir_ref, t, k, w, vir_flag) for k in range(3))
            o_low, o_own, o_high = (part(occ_ref, t, k, w, occ_flag) for k in range(3))
            below_own, below_up = got(up_ref, t, one), got(up_ref, t, two)
            below_occ = got(up_ref, times + t // 2, (one, two)[t % 2])
            above_down, above_own, above_occ = (got(down_ref, 3 * t + n) for n in range(3))

            def cols(slot):
                return slice((slot * times + t) * w, (slot * times + t + 1) * w)

            left_w[:, cols(0)] = v_low.T
            left_w[:, cols(1)] = below_up
            right_w[:w, cols(0)] = v_own.T
            right_w[w:, cols(0)] = v_high.T
            right_w[:w, cols(1)] = v_own
            right_w[w:, cols(1)] = above_down
            right_w[:w, cols(2)] = above_down.T
            right_w[w:, cols(2)] = above_own.T
            low_w[:w, cols(0)] = below_own.T
            low_w[w:, cols(0)] = below_up.T
            low_w[:w, cols(1)] = below_own
            low_w[w:, cols(1)] = v_low

            occ_w[t, 0] = o_own
            occ_w[t, 1] = below_occ
            occ_w[t, 2] = o_low.T
            occ_w[t, 3] = above_occ
            occ_w[t, 4] = o_high.T

    bf = jnp.bfloat16
    for k in range(3):
        block = slice(k * w, (k + 1) * w)
        masked[:, :, block] = kept(flag_ref[0, k], b_ref[:, :, block])

    loops = AUX_STEP // GROUP
    rows = w // loops
    here = pl.ds(pl.multiple_of(step * AUX_STEP, AUX_STEP), AUX_STEP)

    def lay(g, source, target):
        first = pl.multiple_of(g * rows, rows)
        length = rows * source.shape[2]
        at = pl.ds(pl.multiple_of(g * length, length), length)
        target(at, flat(source[:, pl.ds(first, rows), :]))

    def to_own(t):
        def store(at, value):
            flat_own[t, here, at] = value

        return store

    def to_b(at, value):
        flat_b[here, at] = value

    def to_out(ref, slot):
        def store(at, value):
            ref[slot, :, at] = value

        return store

    def virtual_phase(g):
        group = pl.ds(g * GROUP, GROUP)
        lhs = masked[group].reshape(GROUP * w, 3 * w)
        from_left = dot(lhs[:, :w], left_w[...])
        from_right = dot(lhs[:, w:], right_w[...])
        from_low = dot(lhs[:, : 2 * w], low_w[...])

        def piece(product, slot, t):
            return product[:, (slot * times + t) * w : (slot * times + t + 1) * w]

        def put(ref, t, lanes, value):
            ref[t, group, :, lanes] = value.astype(bf).reshape(GROUP, w, w)

        one, two, three = slice(None, w), slice(w, 2 * w), slice(2 * w, None)
        for t in range(times):
            left_c, left_b = piece(from_left, 0, t), piece(from_left, 1, t)
            put(u, t, one, piece(from_low, 0, t))
            put(u, t, two, piece(from_right, 0, t) + left_c)
            put(u, t, three, piece(from_right, 2, t))
            put(x, t, one, piece(from_low, 1, t))
            put(x, t, two, piece(from_right, 1, t) + left_b)
            put(left, t, one, left_c)
            put(left, t, two, left_b)

    def pairs(g):
        return [(g * GROUP + j, g * GROUP + j + 1) for j in range(0, GROUP, 2)]

    def in_pair(occ, source, lanes, target, lanes_to, p, q):
        both = dot(occ, jnp.concatenate([source[p, :, lanes], source[q, :, lanes]], axis=1))
        both = both.astype(bf)
        target[p, :, lanes_to] = both[:, :w]
        target[q, :, lanes_to] = both[:, w:]

    def own_phase(t, g):
        occ = occ_w[t, 0:2].reshape(2 * w, w)
        for j in range(GROUP):
            p = g * GROUP + j
            both = dot(occ, u[t, p, :, : 2 * w]).astype(bf)
            own_n[t, p, :, : 2 * w] = both[:w]
            wide_n[t, p] = both[w:]
        last = slice(2 * w, 3 * w)
        for p, q in pairs(g):
            in_pair(occ_w[t, 0], u.at[t], last, own_n.at[t], last, p, q)

    def other_phase(t, g):
        for j in range(GROUP):
            p = g * GROUP + j
            wide_n[times + t, p] = dot(occ_w[t, 2], x[t, p]).astype(bf)
        for p, q in pairs(g):
            every = slice(None)
            in_pair(occ_w[t, 3], left.at[t], slice(None, w), thin_n.at[t], every, p, q)
            in_pair(occ_w[t, 4], left.at[t], slice(w, None), thin_n.at[times + t], every, p, q)

    def lay_b(g):
        lay(g, masked, to_b)

    def lay_own(t, g):
        lay(g, own_n.at[t], to_own(t))
        lay(g, wide_n.at[t], to_out(wide_ref, t))

    def lay_other(t, g):
        lay(g, wide_n.at[times + t], to_out(wide_ref, times + t))
        lay(g, thin_n.at[t], to_out(thin_ref, t))
        lay(g, thin_n.at[times + t], to_out(thin_ref, times + t))

    work, laying = [virtual_phase], [lay_b]
    for t in range(times):
        work += [functools.partial(own_phase, t), functools.partial(other_phase, t)]
        laying += [functools.partial(lay_own, t), functools.partial(lay_other, t)]
    for n, phase in enumerate(work):

        def both(g, carry, phase=phase, before=laying[n - 1] if n else None):
            phase(g)
            if before is not None:
                before(g)
            return carry

        lax.fori_loop(0, loops, both, 0)
    for g in range(loops):
        laying[-1](g)

    @pl.when(step == pl.num_programs(0) - 1)
    def add_up():
        count = times * flat_own.shape[1]
        length = flat_own.shape[2]
        share = length // 8
        total = None
        for n in range(8):
            at = slice(n * share, (n + 1) * share)
            term = dot_nt(flat_own[:, :, at].reshape(count, share), flat_b[:, at])
            total = term if total is None else total + term
        sum_ref[...] = total


def own_terms(tensor, flag, occ, vir, occ_flag, vir_flag, up, down):
    aux, w, band = tensor.shape
    times = occ.shape[0]
    bf = jnp.bfloat16
    x_head, l_head = heads(times, w, CUTS[0][1])

    def whole(shape):
        return pl.BlockSpec(shape, lambda i: (0, 0, 0))

    flops = 2 * aux * w * w * w * (14 * times + 9 * times)
    return pl.pallas_call(
        functools.partial(own_kernel, times, w),
        grid=(aux // AUX_STEP,),
        in_specs=[
            pl.BlockSpec((AUX_STEP, w, band), lambda i: (i, 0, 0)),
            SMEM, whole(occ.shape), whole(vir.shape), SMEM, SMEM,
            whole((x_head, *up.shape[1:])), whole((l_head, *down.shape[1:])),
        ],
        out_specs=[
            pl.BlockSpec((times * aux, aux), lambda i: (0, 0)),
            pl.BlockSpec((2 * times, AUX_STEP, 2 * w * w), lambda i: (0, i, 0)),
            pl.BlockSpec((2 * times, AUX_STEP, w * w), lambda i: (0, i, 0)),
        ],
        out_shape=[
            jax.ShapeDtypeStruct((times * aux, aux), jnp.float32),
            jax.ShapeDtypeStruct((2 * times, aux, 2 * w * w), bf),
            jax.ShapeDtypeStruct((2 * times, aux, w * w), bf),
        ],
        scratch_shapes=[
            pltpu.VMEM((w, 2 * times * w), bf),
            pltpu.VMEM((2 * w, 3 * times * w), bf),
            pltpu.VMEM((2 * w, 2 * times * w), bf),
            pltpu.VMEM((times, 5, w, w), bf),
            pltpu.VMEM((AUX_STEP, w, band), bf),
            pltpu.VMEM((times, AUX_STEP, w, band), bf),
            pltpu.VMEM((times, AUX_STEP, w, 2 * w), bf),
            pltpu.VMEM((times, AUX_STEP, w, 2 * w), bf),
            pltpu.VMEM((times, AUX_STEP, w, band), bf),
            pltpu.VMEM((2 * times, AUX_STEP, w, 2 * w), bf),
            pltpu.VMEM((2 * times, AUX_STEP, w, w), bf),
            pltpu.VMEM((times, aux, w * band), bf),
            pltpu.VMEM((aux, w * band), bf),
        ],
        compiler_params=pltpu.CompilerParams(vmem_limit_bytes=VMEM_LIMIT),
        cost_estimate=pl.CostEstimate(flops=20 * flops, bytes_accessed=800_000_000, transcendentals=0),
        name="own_terms",
    )(tensor, flag, occ, vir, occ_flag, vir_flag, up, down)


def near_kernel(begin, steps, skips, earlier, wide_hbm, thin_hbm, x_hbm, l_hbm, *rest):
    before, rest = rest[:earlier], rest[earlier:]
    out_ref, wide, thin, x, l, held, sems, held_sems = rest
    slots, aux, w = wide.shape[1], wide.shape[2], l.shape[3]
    times = slots // 2

    def copies(s):
        rows = pl.ds(s * ROW_STEP, ROW_STEP)
        far = begin + s * ROW_STEP
        return [
            pltpu.make_async_copy(
                wide_hbm.at[:, :, pl.ds(far * 2 * w, ROW_STEP * 2 * w)], wide.at[s], sems.at[s, 0]
            ),
            pltpu.make_async_copy(
                thin_hbm.at[:, :, pl.ds(far * w, ROW_STEP * w)], thin.at[s], sems.at[s, 1]
            ),
            pltpu.make_async_copy(x_hbm.at[pl.ds(skips[0], aux), rows], x.at[s], sems.at[s, 2]),
            pltpu.make_async_copy(l_hbm.at[pl.ds(skips[1], aux), rows], l.at[s], sems.at[s, 3]),
        ]

    fetch = []
    for n, ref in enumerate(before):
        size = ref.shape[0]
        fetch.append(
            pltpu.make_async_copy(ref, held.at[n, pl.ds(0, size)], held_sems.at[n])
        )
    for s in range(steps):
        for copy in copies(s):
            copy.start()
    for copy in fetch:
        copy.start()
    total = None
    for s in range(steps):
        for copy in copies(s):
            copy.wait()
        wide_s = wide[s].reshape(slots * aux, ROW_STEP * 2 * w)
        thin_s = thin[s].reshape(slots * aux, ROW_STEP * w)
        term = dot_nt(wide_s, flat(x[s])) + dot_nt(thin_s, flat(l[s]))
        total = term if total is None else total + term
    if not earlier:
        out_ref[...] = total
        return
    for copy in fetch:
        copy.wait()
    half = times * aux
    for n in range(1, earlier):
        total = total + held[n]
    for t in range(times):
        rows = slice(t * aux, (t + 1) * aux)
        out_ref[rows] = held[0, rows] + total[rows] + total[half + t * aux : half + (t + 1) * aux].T


def near_sum(wide, thin, x, l, begin, rows, before=()):
    slots, aux, _ = wide.shape
    w = l.shape[2]
    steps = rows // ROW_STEP
    skips = (x.shape[0] - aux, l.shape[0] - aux)
    shape = (slots // 2 * aux if before else slots * aux, aux)
    bf = jnp.bfloat16
    return pl.pallas_call(
        functools.partial(near_kernel, begin, steps, skips, len(before)),
        in_specs=[HBM] * (4 + len(before)),
        out_specs=pl.BlockSpec(memory_space=pltpu.VMEM),
        out_shape=jax.ShapeDtypeStruct(shape, jnp.float32),
        scratch_shapes=[
            pltpu.VMEM((steps, slots, aux, ROW_STEP * 2 * w), bf),
            pltpu.VMEM((steps, slots, aux, ROW_STEP * w), bf),
            pltpu.VMEM((steps, aux, ROW_STEP, 2 * w), bf),
            pltpu.VMEM((steps, aux, ROW_STEP, w), bf),
            pltpu.VMEM((max(len(before), 1), slots * aux, aux), jnp.float32),
            pltpu.SemaphoreType.DMA((steps, 4)),
            pltpu.SemaphoreType.DMA((max(len(before), 1),)),
        ],
        compiler_params=pltpu.CompilerParams(vmem_limit_bytes=VMEM_LIMIT),
        cost_estimate=pl.CostEstimate(
            flops=2 * slots * aux * aux * rows * 3 * w,
            bytes_accessed=2 * (slots + 1) * aux * rows * 3 * w,
            transcendentals=0,
        ),
        name="near_sum",
    )(wide, thin, x, l, *before)


def scattered_sum(value, axis):
    count = lax.axis_size(axis)
    me = lax.axis_index(axis)
    share = value.shape[0] // count
    if count & (count - 1):
        return lax.dynamic_slice_in_dim(lax.psum(value, axis), me * share, share, 0)
    bits = count.bit_length() - 1
    current = value.reshape((2,) * bits + (share, value.shape[1]))
    left = list(range(bits))
    while left:
        chosen = left[-2:]

        def pick(flips):
            block = current
            for bit in chosen:
                dim = len(left) - 1 - left.index(bit)
                at = ((me >> bit) & 1) ^ ((flips >> bit) & 1)
                block = lax.dynamic_slice_in_dim(block, at, 1, dim)
            return block.reshape((2,) * (len(left) - len(chosen)) + (share, value.shape[1]))

        total = pick(0)
        for code in range(1, 1 << len(chosen)):
            flips = sum(((code >> j) & 1) << bit for j, bit in enumerate(chosen))
            pairs = [(i, i ^ flips) for i in range(count)]
            total = total + lax.ppermute(pick(flips), axis, pairs)
        current = total
        left = left[: len(left) - len(chosen)]
    return current


def body(tensor, tensor_mask, occupied, occupied_mask, virtual, virtual_mask):
    count = lax.axis_size("orb")
    forward = [(i, i + 1) for i in range(count - 1)]
    backward = [(i + 1, i) for i in range(count - 1)]

    arrived = []
    source = tensor
    for begin, rows in CUTS:
        if not arrived:
            x, l = first_cut(
                tensor, tensor_mask, occupied, virtual, occupied_mask, virtual_mask
            )
        else:
            x, l = later_cut(source, tensor_mask, begin, rows)
        source, x, l = lax.optimization_barrier((source, x, l))
        if arrived:
            x, l, *arrived[0] = lax.optimization_barrier((x, l, *arrived[0]))
        arrived.append([lax.ppermute(x, "orb", forward), lax.ppermute(l, "orb", backward)])

    total, wide, thin = own_terms(
        tensor, tensor_mask, occupied, virtual, occupied_mask, virtual_mask, *arrived[0]
    )
    before = [total]
    for (begin, rows), (x, l) in zip(CUTS, arrived, strict=True):
        last = len(before) == len(CUTS)
        before.append(near_sum(wide, thin, x, l, begin, rows, before if last else ()))
    return scattered_sum(before[-1], "orb")


def solution(mesh):
    return jax.shard_map(
        body,
        mesh=mesh,
        in_specs=(
            P("grp", "orb", None),
            P("orb", "grp"),
            P("grp", "orb", None),
            P("grp", "orb", None),
            P("grp", "orb", None),
            P("grp", "orb", None),
        ),
        out_specs=P("orb", "grp"),
        check_vma=False,
    )
```

```python
import functools
import math

import jax
import jax.numpy as jnp
from jax import lax
from jax.experimental import pallas as pl
from jax.experimental.pallas import tpu as pltpu
from jax.sharding import PartitionSpec as P

CUTS = ((0, 80), (80, 48))
AUX_STEP = 16
GROUP = 8
ROW_STEP = 16
AHEAD = 2
VMEM_LIMIT = 60 * 1024 * 1024
NEAR_LIMIT = 12 * 1024 * 1024
ANY = pl.BlockSpec(memory_space=pl.ANY)
SMEM = pl.BlockSpec(memory_space=pltpu.SMEM)


def dot(lhs, rhs):
    return jnp.dot(lhs, rhs, preferred_element_type=jnp.float32)


def dot_nt(lhs, rhs):
    return lax.dot_general(
        lhs, rhs, (((1,), (1,)), ((), ())), preferred_element_type=jnp.float32
    )


def flat(block):
    return pltpu.einshape("plc->p(lc)", block)


def kept(flag, block):
    return jnp.where(flag != 0, block, jnp.zeros_like(block))


def part(ref, t, k, width, flag):
    return kept(flag[t, 0, k], ref[t, :, k * width : (k + 1) * width])


def edge_kernel(times, width, occ_ref, vir_ref, occ_flag, vir_flag, up_ref, down_ref):
    w = width
    for t in range(times):
        up_ref[t, :, :w] = part(vir_ref, t, 1, w, vir_flag)
        up_ref[t, :, w : 2 * w] = part(vir_ref, t, 2, w, vir_flag)
        up_ref[t, :, 2 * w :] = part(occ_ref, t, 2, w, occ_flag)
        down_ref[t, :, :w] = part(vir_ref, t, 0, w, vir_flag)
        down_ref[t, :, w : 2 * w] = part(vir_ref, t, 1, w, vir_flag)
        down_ref[t, :, 2 * w :] = part(occ_ref, t, 0, w, occ_flag)


def edges(occ, vir, occ_flag, vir_flag):
    times, w, _ = occ.shape
    whole = pl.BlockSpec(occ.shape, lambda i: (0, 0, 0))
    return pl.pallas_call(
        functools.partial(edge_kernel, times, w),
        grid=(1,),
        in_specs=[whole, whole, SMEM, SMEM],
        out_specs=[whole, whole],
        out_shape=[jax.ShapeDtypeStruct(occ.shape, occ.dtype)] * 2,
        name="edges",
    )(occ, vir, occ_flag, vir_flag)


def cut_kernel(width, b_ref, flag_ref, x_ref, l_ref):
    w = width
    l_ref[...] = kept(flag_ref[0, 0], b_ref[:, :, :w])
    x_ref[:, :, :w] = kept(flag_ref[0, 1], b_ref[:, :, w : 2 * w])
    x_ref[:, :, w:] = kept(flag_ref[0, 2], b_ref[:, :, 2 * w :])


def cut(tensor, flag, begin, rows):
    aux, w, band = tensor.shape
    size = math.gcd(begin, rows)
    step = aux if size <= ROW_STEP else AUX_STEP
    base = begin // size

    def spec(lanes, first):
        return pl.BlockSpec((step, size, lanes), lambda i, j: (i, first + j, 0))

    return pl.pallas_call(
        functools.partial(cut_kernel, w),
        grid=(aux // step, rows // size),
        in_specs=[spec(band, base), SMEM],
        out_specs=[spec(2 * w, 0), spec(w, 0)],
        out_shape=[
            jax.ShapeDtypeStruct((aux, rows, 2 * w), tensor.dtype),
            jax.ShapeDtypeStruct((aux, rows, w), tensor.dtype),
        ],
        compiler_params=pltpu.CompilerParams(vmem_limit_bytes=VMEM_LIMIT),
        name="cut",
    )(tensor, flag)


def own_kernel(
    times, width, b_ref, flag_ref, occ_ref, vir_ref, occ_flag, vir_flag, up_ref, down_ref,
    sum_ref, wide_ref, thin_ref,
    left_w, right_w, low_w, occ_w, masked, u, x, left, own_n, wide_n, thin_n, flat_own, flat_b,
):
    w = width
    step = pl.program_id(0)

    @pl.when(step == 0)
    def build():
        for t in range(times):
            v_low, v_own, v_high = (part(vir_ref, t, k, w, vir_flag) for k in range(3))
            o_low, o_own, o_high = (part(occ_ref, t, k, w, occ_flag) for k in range(3))
            below_own, below_up, below_occ = (
                up_ref[t, :, k * w : (k + 1) * w] for k in range(3)
            )
            above_down, above_own, above_occ = (
                down_ref[t, :, k * w : (k + 1) * w] for k in range(3)
            )

            def cols(slot):
                return slice((slot * times + t) * w, (slot * times + t + 1) * w)

            left_w[:, cols(0)] = v_low.T
            left_w[:, cols(1)] = below_up
            right_w[:w, cols(0)] = v_own.T
            right_w[w:, cols(0)] = v_high.T
            right_w[:w, cols(1)] = v_own
            right_w[w:, cols(1)] = above_down
            right_w[:w, cols(2)] = above_down.T
            right_w[w:, cols(2)] = above_own.T
            low_w[:w, cols(0)] = below_own.T
            low_w[w:, cols(0)] = below_up.T
            low_w[:w, cols(1)] = below_own
            low_w[w:, cols(1)] = v_low

            occ_w[t, 0] = o_own
            occ_w[t, 1] = below_occ
            occ_w[t, 2] = o_low.T
            occ_w[t, 3] = above_occ
            occ_w[t, 4] = o_high.T

    bf = jnp.bfloat16
    for k in range(3):
        block = slice(k * w, (k + 1) * w)
        masked[:, :, block] = kept(flag_ref[0, k], b_ref[:, :, block])

    loops = AUX_STEP // GROUP
    rows = w // loops
    here = pl.ds(pl.multiple_of(step * AUX_STEP, AUX_STEP), AUX_STEP)

    def lay(g, source, target):
        first = pl.multiple_of(g * rows, rows)
        length = rows * source.shape[2]
        at = pl.ds(pl.multiple_of(g * length, length), length)
        target(at, flat(source[:, pl.ds(first, rows), :]))

    def to_own(t):
        def store(at, value):
            flat_own[t, here, at] = value

        return store

    def to_b(at, value):
        flat_b[here, at] = value

    def to_out(ref, slot):
        def store(at, value):
            ref[slot, :, at] = value

        return store

    def virtual_phase(g):
        group = pl.ds(g * GROUP, GROUP)
        lhs = masked[group].reshape(GROUP * w, 3 * w)
        from_left = dot(lhs[:, :w], left_w[...])
        from_right = dot(lhs[:, w:], right_w[...])
        from_low = dot(lhs[:, : 2 * w], low_w[...])

        def piece(product, slot, t):
            return product[:, (slot * times + t) * w : (slot * times + t + 1) * w]

        def put(ref, t, lanes, value):
            ref[t, group, :, lanes] = value.astype(bf).reshape(GROUP, w, w)

        one, two, three = slice(None, w), slice(w, 2 * w), slice(2 * w, None)
        for t in range(times):
            left_c, left_b = piece(from_left, 0, t), piece(from_left, 1, t)
            put(u, t, one, piece(from_low, 0, t))
            put(u, t, two, piece(from_right, 0, t) + left_c)
            put(u, t, three, piece(from_right, 2, t))
            put(x, t, one, piece(from_low, 1, t))
            put(x, t, two, piece(from_right, 1, t) + left_b)
            put(left, t, one, left_c)
            put(left, t, two, left_b)

    def pairs(g):
        return [(g * GROUP + j, g * GROUP + j + 1) for j in range(0, GROUP, 2)]

    def in_pair(occ, source, lanes, target, lanes_to, p, q):
        both = dot(occ, jnp.concatenate([source[p, :, lanes], source[q, :, lanes]], axis=1))
        both = both.astype(bf)
        target[p, :, lanes_to] = both[:, :w]
        target[q, :, lanes_to] = both[:, w:]

    def own_phase(t, g):
        occ = occ_w[t, 0:2].reshape(2 * w, w)
        for j in range(GROUP):
            p = g * GROUP + j
            both = dot(occ, u[t, p, :, : 2 * w]).astype(bf)
            own_n[t, p, :, : 2 * w] = both[:w]
            wide_n[t, p] = both[w:]
        last = slice(2 * w, 3 * w)
        for p, q in pairs(g):
            in_pair(occ_w[t, 0], u.at[t], last, own_n.at[t], last, p, q)

    def other_phase(t, g):
        for j in range(GROUP):
            p = g * GROUP + j
            wide_n[times + t, p] = dot(occ_w[t, 2], x[t, p]).astype(bf)
        for p, q in pairs(g):
            every = slice(None)
            in_pair(occ_w[t, 3], left.at[t], slice(None, w), thin_n.at[t], every, p, q)
            in_pair(occ_w[t, 4], left.at[t], slice(w, None), thin_n.at[times + t], every, p, q)

    def lay_b(g):
        lay(g, masked, to_b)

    def lay_own(t, g):
        lay(g, own_n.at[t], to_own(t))
        lay(g, wide_n.at[t], to_out(wide_ref, t))

    def lay_other(t, g):
        lay(g, wide_n.at[times + t], to_out(wide_ref, times + t))
        lay(g, thin_n.at[t], to_out(thin_ref, t))
        lay(g, thin_n.at[times + t], to_out(thin_ref, times + t))

    work, laying = [virtual_phase], [lay_b]
    for t in range(times):
        work += [functools.partial(own_phase, t), functools.partial(other_phase, t)]
        laying += [functools.partial(lay_own, t), functools.partial(lay_other, t)]
    for n, phase in enumerate(work):

        def both(g, phase=phase, before=laying[n - 1] if n else None):
            phase(g)
            if before is not None:
                before(g)

        for g in range(loops):
            both(g)
    for g in range(loops):
        laying[-1](g)

    @pl.when(step == pl.num_programs(0) - 1)
    def add_up():
        count = times * flat_own.shape[1]
        length = flat_own.shape[2]
        share = length // 8
        total = None
        for n in range(8):
            at = slice(n * share, (n + 1) * share)
            term = dot_nt(flat_own[:, :, at].reshape(count, share), flat_b[:, at])
            total = term if total is None else total + term
        sum_ref[...] = total


def own_terms(tensor, flag, occ, vir, occ_flag, vir_flag, up, down):
    aux, w, band = tensor.shape
    times = occ.shape[0]
    bf = jnp.bfloat16
    whole = pl.BlockSpec(occ.shape, lambda i: (0, 0, 0))

    flops = 2 * aux * w * w * w * (14 * times + 9 * times)
    return pl.pallas_call(
        functools.partial(own_kernel, times, w),
        grid=(aux // AUX_STEP,),
        in_specs=[
            pl.BlockSpec((AUX_STEP, w, band), lambda i: (i, 0, 0)),
            SMEM, whole, whole, SMEM, SMEM, whole, whole,
        ],
        out_specs=[
            pl.BlockSpec((times * aux, aux), lambda i: (0, 0)),
            pl.BlockSpec((2 * times, AUX_STEP, 2 * w * w), lambda i: (0, i, 0)),
            pl.BlockSpec((2 * times, AUX_STEP, w * w), lambda i: (0, i, 0)),
        ],
        out_shape=[
            jax.ShapeDtypeStruct((times * aux, aux), jnp.float32),
            jax.ShapeDtypeStruct((2 * times, aux, 2 * w * w), bf),
            jax.ShapeDtypeStruct((2 * times, aux, w * w), bf),
        ],
        scratch_shapes=[
            pltpu.VMEM((w, 2 * times * w), bf),
            pltpu.VMEM((2 * w, 3 * times * w), bf),
            pltpu.VMEM((2 * w, 2 * times * w), bf),
            pltpu.VMEM((times, 5, w, w), bf),
            pltpu.VMEM((AUX_STEP, w, band), bf),
            pltpu.VMEM((times, AUX_STEP, w, band), bf),
            pltpu.VMEM((times, AUX_STEP, w, 2 * w), bf),
            pltpu.VMEM((times, AUX_STEP, w, 2 * w), bf),
            pltpu.VMEM((times, AUX_STEP, w, band), bf),
            pltpu.VMEM((2 * times, AUX_STEP, w, 2 * w), bf),
            pltpu.VMEM((2 * times, AUX_STEP, w, w), bf),
            pltpu.VMEM((times, aux, w * band), bf),
            pltpu.VMEM((aux, w * band), bf),
        ],
        compiler_params=pltpu.CompilerParams(vmem_limit_bytes=VMEM_LIMIT),
        cost_estimate=pl.CostEstimate(flops=flops // 50, bytes_accessed=1_000_000, transcendentals=0),
        name="own_terms",
    )(tensor, flag, occ, vir, occ_flag, vir_flag, up, down)


def hold_kernel(parts, wide_hbm, thin_hbm, wide_ref, thin_ref, sems):
    copies = []
    for n, (source, target) in enumerate(((wide_hbm, wide_ref), (thin_hbm, thin_ref))):
        share = source.shape[2] // parts
        for j in range(parts):
            at = pl.ds(j * share, share)
            copies.append(
                pltpu.make_async_copy(source.at[:, :, at], target.at[:, :, at], sems.at[n, j])
            )
    for copy in copies:
        copy.start()
    for copy in copies:
        copy.wait()


def hold(wide, thin):
    parts = 4
    return pl.pallas_call(
        functools.partial(hold_kernel, parts),
        in_specs=[ANY, ANY],
        out_specs=[pl.BlockSpec(memory_space=pltpu.VMEM)] * 2,
        out_shape=[pltpu.VMEM(wide.shape, wide.dtype), pltpu.VMEM(thin.shape, thin.dtype)],
        scratch_shapes=[pltpu.SemaphoreType.DMA((2, parts))],
        compiler_params=pltpu.CompilerParams(vmem_limit_bytes=NEAR_LIMIT),
        name="hold",
    )(wide, thin)


def in_vmem(value):
    return pltpu.with_memory_space_constraint(value, pltpu.VMEM)


def near_kernel(begin, steps, earlier, wide, thin, x_hbm, l_hbm, *rest):
    before, rest = rest[:earlier], rest[earlier:]
    out_ref, x, l, total, held, sems, held_sems = rest
    slots, aux, w = wide.shape[0], wide.shape[1], l.shape[3]
    times = slots // 2

    def copies(s):
        rows = pl.ds(s * ROW_STEP, ROW_STEP)
        return [
            pltpu.make_async_copy(x_hbm.at[:, rows], x.at[s], sems.at[s, 0]),
            pltpu.make_async_copy(l_hbm.at[:, rows], l.at[s], sems.at[s, 1]),
        ]

    fetch = []
    for n, ref in enumerate(before):
        size = ref.shape[0]
        fetch.append(
            pltpu.make_async_copy(ref, held.at[n, pl.ds(0, size)], held_sems.at[n])
        )
    for s in range(min(AHEAD, steps)):
        for copy in copies(s):
            copy.start()
    for copy in fetch:
        copy.start()
    total[...] = jnp.zeros_like(total)
    for s in range(steps):
        if s + AHEAD < steps:
            for copy in copies(s + AHEAD):
                copy.start()
        for copy in copies(s):
            copy.wait()
        far = begin + s * ROW_STEP
        wide_s = wide[:, :, far * 2 * w : (far + ROW_STEP) * 2 * w]
        thin_s = thin[:, :, far * w : (far + ROW_STEP) * w]
        total[...] += dot_nt(wide_s.reshape(slots * aux, ROW_STEP * 2 * w), flat(x[s])) + dot_nt(
            thin_s.reshape(slots * aux, ROW_STEP * w), flat(l[s])
        )
    if not earlier:
        out_ref[...] = total[...]
        return
    for copy in fetch:
        copy.wait()
    half = times * aux
    for n in range(1, earlier):
        total[...] += held[n]
    for t in range(times):
        rows = slice(t * aux, (t + 1) * aux)
        out_ref[rows] = held[0, rows] + total[rows] + total[half + t * aux : half + (t + 1) * aux].T


def near_sum(wide, thin, x, l, begin, rows, before=()):
    slots, aux, _ = wide.shape
    w = l.shape[2]
    steps = rows // ROW_STEP
    shape = (slots // 2 * aux if before else slots * aux, aux)
    bf = jnp.bfloat16
    vmem = pl.BlockSpec(memory_space=pltpu.VMEM)
    return pl.pallas_call(
        functools.partial(near_kernel, begin, steps, len(before)),
        in_specs=[vmem, vmem] + [ANY] * (2 + len(before)),
        out_specs=vmem,
        out_shape=jax.ShapeDtypeStruct(shape, jnp.float32),
        scratch_shapes=[
            pltpu.VMEM((steps, aux, ROW_STEP, 2 * w), bf),
            pltpu.VMEM((steps, aux, ROW_STEP, w), bf),
            pltpu.VMEM((slots * aux, aux), jnp.float32),
            pltpu.VMEM((max(len(before), 1), slots * aux, aux), jnp.float32),
            pltpu.SemaphoreType.DMA((steps, 2)),
            pltpu.SemaphoreType.DMA((max(len(before), 1),)),
        ],
        compiler_params=pltpu.CompilerParams(vmem_limit_bytes=NEAR_LIMIT),
        cost_estimate=pl.CostEstimate(
            flops=20 * slots * aux * aux * rows * 3 * w,
            bytes_accessed=20 * (slots + 1) * aux * rows * 3 * w,
            transcendentals=0,
        ),
        name="near_sum",
    )(in_vmem(wide), in_vmem(thin), x, l, *before)


def scattered_sum(value, axis):
    count = lax.axis_size(axis)
    me = lax.axis_index(axis)
    share = value.shape[0] // count
    if count & (count - 1):
        return lax.dynamic_slice_in_dim(lax.psum(value, axis), me * share, share, 0)
    bits = count.bit_length() - 1
    current = value.reshape((2,) * bits + (share, value.shape[1]))
    left = list(range(bits))
    while left:
        chosen = left[-2:]

        def pick(flips):
            block = current
            for bit in chosen:
                dim = len(left) - 1 - left.index(bit)
                at = ((me >> bit) & 1) ^ ((flips >> bit) & 1)
                block = lax.dynamic_slice_in_dim(block, at, 1, dim)
            return block.reshape((2,) * (len(left) - len(chosen)) + (share, value.shape[1]))

        total = pick(0)
        for code in range(1, 1 << len(chosen)):
            flips = sum(((code >> j) & 1) << bit for j, bit in enumerate(chosen))
            pairs = [(i, i ^ flips) for i in range(count)]
            total = total + lax.ppermute(pick(flips), axis, pairs)
        current = total
        left = left[: len(left) - len(chosen)]
    return current


def body(tensor, tensor_mask, occupied, occupied_mask, virtual, virtual_mask):
    count = lax.axis_size("orb")
    forward = [(i, i + 1) for i in range(count - 1)]
    backward = [(i + 1, i) for i in range(count - 1)]

    up, down = edges(occupied, virtual, occupied_mask, virtual_mask)
    source, up, down = lax.optimization_barrier((tensor, up, down))
    up = lax.ppermute(up, "orb", forward)
    down = lax.ppermute(down, "orb", backward)
    arrived = []
    for begin, rows in CUTS:
        x, l = cut(source, tensor_mask, begin, rows)
        source, x, l, up, down = lax.optimization_barrier((source, x, l, up, down))
        arrived.append((lax.ppermute(x, "orb", forward), lax.ppermute(l, "orb", backward)))

    total, wide, thin = own_terms(
        tensor, tensor_mask, occupied, virtual, occupied_mask, virtual_mask, up, down
    )
    wide, thin = hold(wide, thin)
    before = [total]
    for (begin, rows), (x, l) in zip(CUTS, arrived, strict=True):
        last = len(before) == len(CUTS)
        before.append(near_sum(wide, thin, x, l, begin, rows, before if last else ()))
    return scattered_sum(before[-1], "orb")


def solution(mesh):
    return jax.shard_map(
        body,
        mesh=mesh,
        in_specs=(
            P("grp", "orb", None),
            P("orb", "grp"),
            P("grp", "orb", None),
            P("grp", "orb", None),
            P("grp", "orb", None),
            P("grp", "orb", None),
        ),
        out_specs=P("orb", "grp"),
        check_vma=False,
    )
```

```python
import functools
import math

import jax
import jax.numpy as jnp
from jax import lax
from jax.experimental import pallas as pl
from jax.experimental.pallas import tpu as pltpu
from jax.sharding import PartitionSpec as P

CUTS = ((0, 80), (80, 48))
AUX_STEP = 16
GROUP = 8
ROW_STEP = 16
AHEAD = 2
VMEM_LIMIT = 60 * 1024 * 1024
NEAR_LIMIT = 12 * 1024 * 1024
ANY = pl.BlockSpec(memory_space=pl.ANY)
SMEM = pl.BlockSpec(memory_space=pltpu.SMEM)


def dot(lhs, rhs):
    return jnp.dot(lhs, rhs, preferred_element_type=jnp.float32)


def dot_nt(lhs, rhs):
    return lax.dot_general(
        lhs, rhs, (((1,), (1,)), ((), ())), preferred_element_type=jnp.float32
    )


def flat(block):
    return pltpu.einshape("plc->p(lc)", block)


def kept(flag, block):
    return jnp.where(flag != 0, block, jnp.zeros_like(block))


def part(ref, t, k, width, flag):
    return kept(flag[t, 0, k], ref[t, :, k * width : (k + 1) * width])


def edge_kernel(times, width, odd_ref, occ_ref, vir_ref, occ_flag, vir_flag, even_pair, odd_pair):
    w = width

    def put(ref, blocks):
        for t in range(times):
            for n, (source, flag, k) in enumerate(blocks):
                ref[t, :, n * w : (n + 1) * w] = part(source, t, k, w, flag)

    vir, occ = (vir_ref, vir_flag), (occ_ref, occ_flag)
    up = [(*vir, 1), (*vir, 2), (*occ, 2)]
    down = [(*vir, 0), (*vir, 1), (*occ, 0)]

    @pl.when(odd_ref[0] == 0)
    def first_of_pair():
        put(even_pair, up)
        put(odd_pair, down)

    @pl.when(odd_ref[0] != 0)
    def second_of_pair():
        put(even_pair, down)
        put(odd_pair, up)


def edges(odd, occ, vir, occ_flag, vir_flag):
    times, w, _ = occ.shape
    whole = pl.BlockSpec(occ.shape, lambda i: (0, 0, 0))
    return pl.pallas_call(
        functools.partial(edge_kernel, times, w),
        grid=(1,),
        in_specs=[SMEM, whole, whole, SMEM, SMEM],
        out_specs=[whole, whole],
        out_shape=[jax.ShapeDtypeStruct(occ.shape, occ.dtype)] * 2,
        name="edges",
    )(odd, occ, vir, occ_flag, vir_flag)


def cut_kernel(width, b_ref, flag_ref, x_ref, l_ref):
    w = width
    l_ref[...] = kept(flag_ref[0, 0], b_ref[:, :, :w])
    x_ref[:, :, :w] = kept(flag_ref[0, 1], b_ref[:, :, w : 2 * w])
    x_ref[:, :, w:] = kept(flag_ref[0, 2], b_ref[:, :, 2 * w :])


def cut(tensor, flag, begin, rows):
    aux, w, band = tensor.shape
    size = math.gcd(begin, rows)
    step = aux if size <= ROW_STEP else AUX_STEP
    base = begin // size

    def spec(lanes, first):
        return pl.BlockSpec((step, size, lanes), lambda i, j: (i, first + j, 0))

    return pl.pallas_call(
        functools.partial(cut_kernel, w),
        grid=(aux // step, rows // size),
        in_specs=[spec(band, base), SMEM],
        out_specs=[spec(2 * w, 0), spec(w, 0)],
        out_shape=[
            jax.ShapeDtypeStruct((aux, rows, 2 * w), tensor.dtype),
            jax.ShapeDtypeStruct((aux, rows, w), tensor.dtype),
        ],
        compiler_params=pltpu.CompilerParams(vmem_limit_bytes=VMEM_LIMIT),
        name="cut",
    )(tensor, flag)


def own_kernel(
    times, width, odd_ref, b_ref, flag_ref, occ_ref, vir_ref, occ_flag, vir_flag, even_pair, odd_pair,
    sum_ref, wide_ref, thin_ref,
    left_w, right_w, low_w, occ_w, masked, u, x, left, own_n, wide_n, thin_n, flat_own, flat_b,
):
    w = width
    step = pl.program_id(0)

    @pl.when(step == 0)
    def build():
        for t in range(times):
            v_low, v_own, v_high = (part(vir_ref, t, k, w, vir_flag) for k in range(3))
            o_low, o_own, o_high = (part(occ_ref, t, k, w, occ_flag) for k in range(3))
            from_even = [even_pair[t, :, k * w : (k + 1) * w] for k in range(3)]
            from_odd = [odd_pair[t, :, k * w : (k + 1) * w] for k in range(3)]
            odd = odd_ref[0] != 0
            below_own, below_up, below_occ = (
                jnp.where(odd, one, two) for one, two in zip(from_even, from_odd, strict=True)
            )
            above_down, above_own, above_occ = (
                jnp.where(odd, two, one) for one, two in zip(from_even, from_odd, strict=True)
            )

            def cols(slot):
                return slice((slot * times + t) * w, (slot * times + t + 1) * w)

            left_w[:, cols(0)] = v_low.T
            left_w[:, cols(1)] = below_up
            right_w[:w, cols(0)] = v_own.T
            right_w[w:, cols(0)] = v_high.T
            right_w[:w, cols(1)] = v_own
            right_w[w:, cols(1)] = above_down
            right_w[:w, cols(2)] = above_down.T
            right_w[w:, cols(2)] = above_own.T
            low_w[:w, cols(0)] = below_own.T
            low_w[w:, cols(0)] = below_up.T
            low_w[:w, cols(1)] = below_own
            low_w[w:, cols(1)] = v_low

            occ_w[t, 0] = o_own
            occ_w[t, 1] = below_occ
            occ_w[t, 2] = o_low.T
            occ_w[t, 3] = above_occ
            occ_w[t, 4] = o_high.T

    bf = jnp.bfloat16
    for k in range(3):
        block = slice(k * w, (k + 1) * w)
        masked[:, :, block] = kept(flag_ref[0, k], b_ref[:, :, block])

    loops = AUX_STEP // GROUP
    rows = w // loops
    here = pl.ds(pl.multiple_of(step * AUX_STEP, AUX_STEP), AUX_STEP)

    def lay(g, source, target):
        first = pl.multiple_of(g * rows, rows)
        length = rows * source.shape[2]
        at = pl.ds(pl.multiple_of(g * length, length), length)
        target(at, flat(source[:, pl.ds(first, rows), :]))

    def to_own(t):
        def store(at, value):
            flat_own[t, here, at] = value

        return store

    def to_b(at, value):
        flat_b[here, at] = value

    def to_out(ref, slot):
        def store(at, value):
            ref[slot, :, at] = value

        return store

    def virtual_phase(g):
        group = pl.ds(g * GROUP, GROUP)
        lhs = masked[group].reshape(GROUP * w, 3 * w)
        from_left = dot(lhs[:, :w], left_w[...])
        from_right = dot(lhs[:, w:], right_w[...])
        from_low = dot(lhs[:, : 2 * w], low_w[...])

        def piece(product, slot, t):
            return product[:, (slot * times + t) * w : (slot * times + t + 1) * w]

        def put(ref, t, lanes, value):
            ref[t, group, :, lanes] = value.astype(bf).reshape(GROUP, w, w)

        one, two, three = slice(None, w), slice(w, 2 * w), slice(2 * w, None)
        for t in range(times):
            left_c, left_b = piece(from_left, 0, t), piece(from_left, 1, t)
            put(u, t, one, piece(from_low, 0, t))
            put(u, t, two, piece(from_right, 0, t) + left_c)
            put(u, t, three, piece(from_right, 2, t))
            put(x, t, one, piece(from_low, 1, t))
            put(x, t, two, piece(from_right, 1, t) + left_b)
            put(left, t, one, left_c)
            put(left, t, two, left_b)

    def pairs(g):
        return [(g * GROUP + j, g * GROUP + j + 1) for j in range(0, GROUP, 2)]

    def in_pair(occ, source, lanes, target, lanes_to, p, q):
        both = dot(occ, jnp.concatenate([source[p, :, lanes], source[q, :, lanes]], axis=1))
        both = both.astype(bf)
        target[p, :, lanes_to] = both[:, :w]
        target[q, :, lanes_to] = both[:, w:]

    def own_phase(t, g):
        occ = occ_w[t, 0:2].reshape(2 * w, w)
        for j in range(GROUP):
            p = g * GROUP + j
            both = dot(occ, u[t, p, :, : 2 * w]).astype(bf)
            own_n[t, p, :, : 2 * w] = both[:w]
            wide_n[t, p] = both[w:]
        last = slice(2 * w, 3 * w)
        for p, q in pairs(g):
            in_pair(occ_w[t, 0], u.at[t], last, own_n.at[t], last, p, q)

    def other_phase(t, g):
        for j in range(GROUP):
            p = g * GROUP + j
            wide_n[times + t, p] = dot(occ_w[t, 2], x[t, p]).astype(bf)
        for p, q in pairs(g):
            every = slice(None)
            in_pair(occ_w[t, 3], left.at[t], slice(None, w), thin_n.at[t], every, p, q)
            in_pair(occ_w[t, 4], left.at[t], slice(w, None), thin_n.at[times + t], every, p, q)

    def lay_b(g):
        lay(g, masked, to_b)

    def lay_own(t, g):
        lay(g, own_n.at[t], to_own(t))
        lay(g, wide_n.at[t], to_out(wide_ref, t))

    def lay_other(t, g):
        lay(g, wide_n.at[times + t], to_out(wide_ref, times + t))
        lay(g, thin_n.at[t], to_out(thin_ref, t))
        lay(g, thin_n.at[times + t], to_out(thin_ref, times + t))

    work, laying = [virtual_phase], [lay_b]
    for t in range(times):
        work += [functools.partial(own_phase, t), functools.partial(other_phase, t)]
        laying += [functools.partial(lay_own, t), functools.partial(lay_other, t)]
    for n, phase in enumerate(work):

        def both(g, phase=phase, before=laying[n - 1] if n else None):
            phase(g)
            if before is not None:
                before(g)

        for g in range(loops):
            both(g)
    for g in range(loops):
        laying[-1](g)

    @pl.when(step == pl.num_programs(0) - 1)
    def add_up():
        count = times * flat_own.shape[1]
        length = flat_own.shape[2]
        share = length // 8
        total = None
        for n in range(8):
            at = slice(n * share, (n + 1) * share)
            term = dot_nt(flat_own[:, :, at].reshape(count, share), flat_b[:, at])
            total = term if total is None else total + term
        sum_ref[...] = total


def own_terms(odd, tensor, flag, occ, vir, occ_flag, vir_flag, even_pair, odd_pair):
    aux, w, band = tensor.shape
    times = occ.shape[0]
    bf = jnp.bfloat16
    whole = pl.BlockSpec(occ.shape, lambda i: (0, 0, 0))

    flops = 2 * aux * w * w * w * (14 * times + 9 * times)
    return pl.pallas_call(
        functools.partial(own_kernel, times, w),
        grid=(aux // AUX_STEP,),
        in_specs=[
            SMEM,
            pl.BlockSpec((AUX_STEP, w, band), lambda i: (i, 0, 0)),
            SMEM, whole, whole, SMEM, SMEM, whole, whole,
        ],
        out_specs=[
            pl.BlockSpec((times * aux, aux), lambda i: (0, 0)),
            pl.BlockSpec((2 * times, AUX_STEP, 2 * w * w), lambda i: (0, i, 0)),
            pl.BlockSpec((2 * times, AUX_STEP, w * w), lambda i: (0, i, 0)),
        ],
        out_shape=[
            jax.ShapeDtypeStruct((times * aux, aux), jnp.float32),
            jax.ShapeDtypeStruct((2 * times, aux, 2 * w * w), bf),
            jax.ShapeDtypeStruct((2 * times, aux, w * w), bf),
        ],
        scratch_shapes=[
            pltpu.VMEM((w, 2 * times * w), bf),
            pltpu.VMEM((2 * w, 3 * times * w), bf),
            pltpu.VMEM((2 * w, 2 * times * w), bf),
            pltpu.VMEM((times, 5, w, w), bf),
            pltpu.VMEM((AUX_STEP, w, band), bf),
            pltpu.VMEM((times, AUX_STEP, w, band), bf),
            pltpu.VMEM((times, AUX_STEP, w, 2 * w), bf),
            pltpu.VMEM((times, AUX_STEP, w, 2 * w), bf),
            pltpu.VMEM((times, AUX_STEP, w, band), bf),
            pltpu.VMEM((2 * times, AUX_STEP, w, 2 * w), bf),
            pltpu.VMEM((2 * times, AUX_STEP, w, w), bf),
            pltpu.VMEM((times, aux, w * band), bf),
            pltpu.VMEM((aux, w * band), bf),
        ],
        compiler_params=pltpu.CompilerParams(vmem_limit_bytes=VMEM_LIMIT),
        cost_estimate=pl.CostEstimate(flops=flops // 50, bytes_accessed=1_000_000, transcendentals=0),
        name="own_terms",
    )(odd, tensor, flag, occ, vir, occ_flag, vir_flag, even_pair, odd_pair)


def hold_kernel(parts, wide_hbm, thin_hbm, wide_ref, thin_ref, sems):
    copies = []
    for n, (source, target) in enumerate(((wide_hbm, wide_ref), (thin_hbm, thin_ref))):
        share = source.shape[2] // parts
        for j in range(parts):
            at = pl.ds(j * share, share)
            copies.append(
                pltpu.make_async_copy(source.at[:, :, at], target.at[:, :, at], sems.at[n, j])
            )
    for copy in copies:
        copy.start()
    for copy in copies:
        copy.wait()


def hold(wide, thin):
    parts = 4
    return pl.pallas_call(
        functools.partial(hold_kernel, parts),
        in_specs=[ANY, ANY],
        out_specs=[pl.BlockSpec(memory_space=pltpu.VMEM)] * 2,
        out_shape=[pltpu.VMEM(wide.shape, wide.dtype), pltpu.VMEM(thin.shape, thin.dtype)],
        scratch_shapes=[pltpu.SemaphoreType.DMA((2, parts))],
        compiler_params=pltpu.CompilerParams(vmem_limit_bytes=NEAR_LIMIT),
        name="hold",
    )(wide, thin)


def in_vmem(value):
    return pltpu.with_memory_space_constraint(value, pltpu.VMEM)


def near_kernel(begin, steps, earlier, wide, thin, x_hbm, l_hbm, *rest):
    before, rest = rest[:earlier], rest[earlier:]
    out_ref, x, l, total, held, sems, held_sems = rest
    slots, aux, w = wide.shape[0], wide.shape[1], l.shape[3]
    times = slots // 2

    def copies(s):
        rows = pl.ds(s * ROW_STEP, ROW_STEP)
        return [
            pltpu.make_async_copy(x_hbm.at[:, rows], x.at[s], sems.at[s, 0]),
            pltpu.make_async_copy(l_hbm.at[:, rows], l.at[s], sems.at[s, 1]),
        ]

    fetch = []
    for n, ref in enumerate(before):
        size = ref.shape[0]
        fetch.append(
            pltpu.make_async_copy(ref, held.at[n, pl.ds(0, size)], held_sems.at[n])
        )
    for s in range(min(AHEAD, steps)):
        for copy in copies(s):
            copy.start()
    for copy in fetch:
        copy.start()
    total[...] = jnp.zeros_like(total)
    for s in range(steps):
        if s + AHEAD < steps:
            for copy in copies(s + AHEAD):
                copy.start()
        for copy in copies(s):
            copy.wait()
        far = begin + s * ROW_STEP
        wide_s = wide[:, :, far * 2 * w : (far + ROW_STEP) * 2 * w]
        thin_s = thin[:, :, far * w : (far + ROW_STEP) * w]
        total[...] += dot_nt(wide_s.reshape(slots * aux, ROW_STEP * 2 * w), flat(x[s])) + dot_nt(
            thin_s.reshape(slots * aux, ROW_STEP * w), flat(l[s])
        )
    if not earlier:
        out_ref[...] = total[...]
        return
    for copy in fetch:
        copy.wait()
    half = times * aux
    for n in range(1, earlier):
        total[...] += held[n]
    for t in range(times):
        rows = slice(t * aux, (t + 1) * aux)
        out_ref[rows] = held[0, rows] + total[rows] + total[half + t * aux : half + (t + 1) * aux].T


def near_sum(wide, thin, x, l, begin, rows, before=()):
    slots, aux, _ = wide.shape
    w = l.shape[2]
    steps = rows // ROW_STEP
    shape = (slots // 2 * aux if before else slots * aux, aux)
    bf = jnp.bfloat16
    vmem = pl.BlockSpec(memory_space=pltpu.VMEM)
    return pl.pallas_call(
        functools.partial(near_kernel, begin, steps, len(before)),
        in_specs=[vmem, vmem] + [ANY] * (2 + len(before)),
        out_specs=vmem,
        out_shape=jax.ShapeDtypeStruct(shape, jnp.float32),
        scratch_shapes=[
            pltpu.VMEM((steps, aux, ROW_STEP, 2 * w), bf),
            pltpu.VMEM((steps, aux, ROW_STEP, w), bf),
            pltpu.VMEM((slots * aux, aux), jnp.float32),
            pltpu.VMEM((max(len(before), 1), slots * aux, aux), jnp.float32),
            pltpu.SemaphoreType.DMA((steps, 2)),
            pltpu.SemaphoreType.DMA((max(len(before), 1),)),
        ],
        compiler_params=pltpu.CompilerParams(vmem_limit_bytes=NEAR_LIMIT),
        cost_estimate=pl.CostEstimate(
            flops=20 * slots * aux * aux * rows * 3 * w,
            bytes_accessed=20 * (slots + 1) * aux * rows * 3 * w,
            transcendentals=0,
        ),
        name="near_sum",
    )(in_vmem(wide), in_vmem(thin), x, l, *before)


def scattered_sum(value, axis):
    count = lax.axis_size(axis)
    me = lax.axis_index(axis)
    share = value.shape[0] // count
    if count & (count - 1):
        return lax.dynamic_slice_in_dim(lax.psum(value, axis), me * share, share, 0)
    bits = count.bit_length() - 1
    current = value.reshape((2,) * bits + (share, value.shape[1]))
    left = list(range(bits))
    while left:
        chosen = left[-2:]

        def pick(flips):
            block = current
            for bit in chosen:
                dim = len(left) - 1 - left.index(bit)
                at = ((me >> bit) & 1) ^ ((flips >> bit) & 1)
                block = lax.dynamic_slice_in_dim(block, at, 1, dim)
            return block.reshape((2,) * (len(left) - len(chosen)) + (share, value.shape[1]))

        total = pick(0)
        for code in reversed(range(1, 1 << len(chosen))):
            flips = sum(((code >> j) & 1) << bit for j, bit in enumerate(chosen))
            pairs = [(i, i ^ flips) for i in range(count)]
            total = total + lax.ppermute(pick(flips), axis, pairs)
        current = total
        left = left[: len(left) - len(chosen)]
    return current


def body(tensor, tensor_mask, occupied, occupied_mask, virtual, virtual_mask):
    count = lax.axis_size("orb")
    forward = [(i, i + 1) for i in range(count - 1)]
    backward = [(i + 1, i) for i in range(count - 1)]

    odd = (lax.axis_index("orb") & 1).astype(jnp.int32).reshape(1)
    even_pair, odd_pair = edges(odd, occupied, virtual, occupied_mask, virtual_mask)
    source, even_pair, odd_pair = lax.optimization_barrier((tensor, even_pair, odd_pair))
    swaps = [[], []]
    for i, j in forward:
        swaps[i % 2] += [(i, j), (j, i)]
    odd_pair = lax.ppermute(odd_pair, "orb", swaps[1])
    even_pair = lax.ppermute(even_pair, "orb", swaps[0])
    arrived = []
    for begin, rows in CUTS:
        x, l = cut(source, tensor_mask, begin, rows)
        source, x, l, even_pair, odd_pair = lax.optimization_barrier(
            (source, x, l, even_pair, odd_pair)
        )
        arrived.append((lax.ppermute(x, "orb", forward), lax.ppermute(l, "orb", backward)))

    total, wide, thin = own_terms(
        odd, tensor, tensor_mask, occupied, virtual, occupied_mask, virtual_mask, even_pair, odd_pair
    )
    wide, thin = hold(wide, thin)
    before = [total]
    for (begin, rows), (x, l) in zip(CUTS, arrived, strict=True):
        last = len(before) == len(CUTS)
        before.append(near_sum(wide, thin, x, l, begin, rows, before if last else ()))
    return scattered_sum(before[-1], "orb")


def solution(mesh):
    return jax.shard_map(
        body,
        mesh=mesh,
        in_specs=(
            P("grp", "orb", None),
            P("orb", "grp"),
            P("grp", "orb", None),
            P("grp", "orb", None),
            P("grp", "orb", None),
            P("grp", "orb", None),
        ),
        out_specs=P("orb", "grp"),
        check_vma=False,
    )
```

```python
import functools

import jax
import jax.numpy as jnp
from jax import lax
from jax.experimental import pallas as pl
from jax.experimental.pallas import tpu as pltpu
from jax.sharding import PartitionSpec as P

CUTS = ((0, 80), (80, 48))
AUX_STEP = 16
GROUP = 8
ROW_STEP = 16
AHEAD = 2
SHARES = 4
VMEM_LIMIT = 60 * 1024 * 1024
NEAR_LIMIT = 12 * 1024 * 1024
ANY = pl.BlockSpec(memory_space=pl.ANY)
HBM = pl.BlockSpec(memory_space=pltpu.HBM)
SMEM = pl.BlockSpec(memory_space=pltpu.SMEM)


def dot(lhs, rhs):
    return jnp.dot(lhs, rhs, preferred_element_type=jnp.float32)


def dot_nt(lhs, rhs):
    return lax.dot_general(
        lhs, rhs, (((1,), (1,)), ((), ())), preferred_element_type=jnp.float32
    )


def flat(block):
    return pltpu.einshape("plc->p(lc)", block)


def kept(flag, block):
    return jnp.where(flag != 0, block, jnp.zeros_like(block))


def part(ref, t, k, width, flag):
    return kept(flag[t, 0, k], ref[t, :, k * width : (k + 1) * width])


def edge_kernel(times, width, odd_ref, occ_ref, vir_ref, occ_flag, vir_flag, even_pair, odd_pair):
    w = width

    def put(ref, blocks):
        for t in range(times):
            for n, (source, flag, k) in enumerate(blocks):
                ref[t, :, n * w : (n + 1) * w] = part(source, t, k, w, flag)

    vir, occ = (vir_ref, vir_flag), (occ_ref, occ_flag)
    up = [(*vir, 1), (*vir, 2), (*occ, 2)]
    down = [(*vir, 0), (*vir, 1), (*occ, 0)]

    @pl.when(odd_ref[0] == 0)
    def first_of_pair():
        put(even_pair, up)
        put(odd_pair, down)

    @pl.when(odd_ref[0] != 0)
    def second_of_pair():
        put(even_pair, down)
        put(odd_pair, up)


def edges(odd, occ, vir, occ_flag, vir_flag):
    times, w, _ = occ.shape
    whole = pl.BlockSpec(occ.shape, lambda i: (0, 0, 0))
    return pl.pallas_call(
        functools.partial(edge_kernel, times, w),
        grid=(1,),
        in_specs=[SMEM, whole, whole, SMEM, SMEM],
        out_specs=[whole, whole],
        out_shape=[jax.ShapeDtypeStruct(occ.shape, occ.dtype)] * 2,
        name="edges",
    )(odd, occ, vir, occ_flag, vir_flag)


def cut_kernel(blocks, begin, rows, width, b_hbm, flag_ref, out_hbm, zeros, sems):
    w = width
    group = out_hbm.shape[0] // SHARES
    zeros[...] = jnp.zeros_like(zeros)

    def copy(n, j, dropped):
        aux = pl.ds(j * group, group)
        source = b_hbm.at[aux, pl.ds(begin, rows), pl.ds(blocks[n] * w, w)]
        target = out_hbm.at[aux, :, pl.ds(n * w, w)]
        return pltpu.make_async_copy(zeros if dropped else source, target, sems.at[n, j])

    for n, k in enumerate(blocks):
        for j in range(SHARES):

            @pl.when(flag_ref[0, k] != 0)
            def keep(n=n, j=j):
                copy(n, j, False).start()

            @pl.when(flag_ref[0, k] == 0)
            def drop(n=n, j=j):
                copy(n, j, True).start()

    for n in range(len(blocks)):
        for j in range(SHARES):
            copy(n, j, False).wait()


def cut(tensor, flag, blocks, begin, rows):
    aux, w, _ = tensor.shape
    return pl.pallas_call(
        functools.partial(cut_kernel, blocks, begin, rows, w),
        in_specs=[HBM, SMEM],
        out_specs=HBM,
        out_shape=jax.ShapeDtypeStruct((aux, rows, len(blocks) * w), tensor.dtype),
        scratch_shapes=[
            pltpu.VMEM((aux // SHARES, rows, w), tensor.dtype),
            pltpu.SemaphoreType.DMA((len(blocks), SHARES)),
        ],
        compiler_params=pltpu.CompilerParams(vmem_limit_bytes=VMEM_LIMIT),
        name="cut",
    )(tensor, flag)


def own_kernel(
    times, width, odd_ref, b_ref, flag_ref, occ_ref, vir_ref, occ_flag, vir_flag, even_pair, odd_pair,
    sum_ref, wide_ref, thin_ref,
    left_w, right_w, low_w, occ_w, masked, u, x, left, own_n, wide_n, thin_n, flat_own, flat_b,
):
    w = width
    step = pl.program_id(0)

    @pl.when(step == 0)
    def build():
        for t in range(times):
            v_low, v_own, v_high = (part(vir_ref, t, k, w, vir_flag) for k in range(3))
            o_low, o_own, o_high = (part(occ_ref, t, k, w, occ_flag) for k in range(3))
            from_even = [even_pair[t, :, k * w : (k + 1) * w] for k in range(3)]
            from_odd = [odd_pair[t, :, k * w : (k + 1) * w] for k in range(3)]
            odd = odd_ref[0] != 0
            below_own, below_up, below_occ = (
                jnp.where(odd, one, two) for one, two in zip(from_even, from_odd, strict=True)
            )
            above_down, above_own, above_occ = (
                jnp.where(odd, two, one) for one, two in zip(from_even, from_odd, strict=True)
            )

            def cols(slot):
                return slice((slot * times + t) * w, (slot * times + t + 1) * w)

            left_w[:, cols(0)] = v_low.T
            left_w[:, cols(1)] = below_up
            right_w[:w, cols(0)] = v_own.T
            right_w[w:, cols(0)] = v_high.T
            right_w[:w, cols(1)] = v_own
            right_w[w:, cols(1)] = above_down
            right_w[:w, cols(2)] = above_down.T
            right_w[w:, cols(2)] = above_own.T
            low_w[:w, cols(0)] = below_own.T
            low_w[w:, cols(0)] = below_up.T
            low_w[:w, cols(1)] = below_own
            low_w[w:, cols(1)] = v_low

            occ_w[t, 0] = o_own
            occ_w[t, 1] = below_occ
            occ_w[t, 2] = o_low.T
            occ_w[t, 3] = above_occ
            occ_w[t, 4] = o_high.T

    bf = jnp.bfloat16
    for k in range(3):
        block = slice(k * w, (k + 1) * w)
        masked[:, :, block] = kept(flag_ref[0, k], b_ref[:, :, block])

    loops = AUX_STEP // GROUP
    rows = w // loops
    here = pl.ds(pl.multiple_of(step * AUX_STEP, AUX_STEP), AUX_STEP)

    def lay(g, source, target):
        first = pl.multiple_of(g * rows, rows)
        length = rows * source.shape[2]
        at = pl.ds(pl.multiple_of(g * length, length), length)
        target(at, flat(source[:, pl.ds(first, rows), :]))

    def to_own(t):
        def store(at, value):
            flat_own[t, here, at] = value

        return store

    def to_b(at, value):
        flat_b[here, at] = value

    def to_out(ref, slot):
        def store(at, value):
            ref[slot, :, at] = value

        return store

    def virtual_phase(g):
        group = pl.ds(g * GROUP, GROUP)
        lhs = masked[group].reshape(GROUP * w, 3 * w)
        from_left = dot(lhs[:, :w], left_w[...])
        from_right = dot(lhs[:, w:], right_w[...])
        from_low = dot(lhs[:, : 2 * w], low_w[...])

        def piece(product, slot, t):
            return product[:, (slot * times + t) * w : (slot * times + t + 1) * w]

        def put(ref, t, lanes, value):
            ref[t, group, :, lanes] = value.astype(bf).reshape(GROUP, w, w)

        one, two, three = slice(None, w), slice(w, 2 * w), slice(2 * w, None)
        for t in range(times):
            left_c, left_b = piece(from_left, 0, t), piece(from_left, 1, t)
            put(u, t, one, piece(from_low, 0, t))
            put(u, t, two, piece(from_right, 0, t) + left_c)
            put(u, t, three, piece(from_right, 2, t))
            put(x, t, one, piece(from_low, 1, t))
            put(x, t, two, piece(from_right, 1, t) + left_b)
            put(left, t, one, left_c)
            put(left, t, two, left_b)

    def pairs(g):
        return [(g * GROUP + j, g * GROUP + j + 1) for j in range(0, GROUP, 2)]

    def in_pair(occ, source, lanes, target, lanes_to, p, q):
        both = dot(occ, jnp.concatenate([source[p, :, lanes], source[q, :, lanes]], axis=1))
        both = both.astype(bf)
        target[p, :, lanes_to] = both[:, :w]
        target[q, :, lanes_to] = both[:, w:]

    def own_phase(t, g):
        occ = occ_w[t, 0:2].reshape(2 * w, w)
        for j in range(GROUP):
            p = g * GROUP + j
            both = dot(occ, u[t, p, :, : 2 * w]).astype(bf)
            own_n[t, p, :, : 2 * w] = both[:w]
            wide_n[t, p] = both[w:]
        last = slice(2 * w, 3 * w)
        for p, q in pairs(g):
            in_pair(occ_w[t, 0], u.at[t], last, own_n.at[t], last, p, q)

    def other_phase(t, g):
        for j in range(GROUP):
            p = g * GROUP + j
            wide_n[times + t, p] = dot(occ_w[t, 2], x[t, p]).astype(bf)
        for p, q in pairs(g):
            every = slice(None)
            in_pair(occ_w[t, 3], left.at[t], slice(None, w), thin_n.at[t], every, p, q)
            in_pair(occ_w[t, 4], left.at[t], slice(w, None), thin_n.at[times + t], every, p, q)

    def lay_b(g):
        lay(g, masked, to_b)

    def lay_own(t, g):
        lay(g, own_n.at[t], to_own(t))
        lay(g, wide_n.at[t], to_out(wide_ref, t))

    def lay_other(t, g):
        lay(g, wide_n.at[times + t], to_out(wide_ref, times + t))
        lay(g, thin_n.at[t], to_out(thin_ref, t))
        lay(g, thin_n.at[times + t], to_out(thin_ref, times + t))

    work, laying = [virtual_phase], [lay_b]
    for t in range(times):
        work += [functools.partial(own_phase, t), functools.partial(other_phase, t)]
        laying += [functools.partial(lay_own, t), functools.partial(lay_other, t)]
    for n, phase in enumerate(work):

        def both(g, phase=phase, before=laying[n - 1] if n else None):
            phase(g)
            if before is not None:
                before(g)

        for g in range(loops):
            both(g)
    for g in range(loops):
        laying[-1](g)

    @pl.when(step == pl.num_programs(0) - 1)
    def add_up():
        count = times * flat_own.shape[1]
        length = flat_own.shape[2]
        share = length // 8
        total = None
        for n in range(8):
            at = slice(n * share, (n + 1) * share)
            term = dot_nt(flat_own[:, :, at].reshape(count, share), flat_b[:, at])
            total = term if total is None else total + term
        sum_ref[...] = total


def own_terms(odd, tensor, flag, occ, vir, occ_flag, vir_flag, even_pair, odd_pair):
    aux, w, band = tensor.shape
    times = occ.shape[0]
    bf = jnp.bfloat16
    whole = pl.BlockSpec(occ.shape, lambda i: (0, 0, 0))

    flops = 2 * aux * w * w * w * (14 * times + 9 * times)
    return pl.pallas_call(
        functools.partial(own_kernel, times, w),
        grid=(aux // AUX_STEP,),
        in_specs=[
            SMEM,
            pl.BlockSpec((AUX_STEP, w, band), lambda i: (i, 0, 0)),
            SMEM, whole, whole, SMEM, SMEM, whole, whole,
        ],
        out_specs=[
            pl.BlockSpec((times * aux, aux), lambda i: (0, 0)),
            pl.BlockSpec((2 * times, AUX_STEP, 2 * w * w), lambda i: (0, i, 0)),
            pl.BlockSpec((2 * times, AUX_STEP, w * w), lambda i: (0, i, 0)),
        ],
        out_shape=[
            jax.ShapeDtypeStruct((times * aux, aux), jnp.float32),
            jax.ShapeDtypeStruct((2 * times, aux, 2 * w * w), bf),
            jax.ShapeDtypeStruct((2 * times, aux, w * w), bf),
        ],
        scratch_shapes=[
            pltpu.VMEM((w, 2 * times * w), bf),
            pltpu.VMEM((2 * w, 3 * times * w), bf),
            pltpu.VMEM((2 * w, 2 * times * w), bf),
            pltpu.VMEM((times, 5, w, w), bf),
            pltpu.VMEM((AUX_STEP, w, band), bf),
            pltpu.VMEM((times, AUX_STEP, w, band), bf),
            pltpu.VMEM((times, AUX_STEP, w, 2 * w), bf),
            pltpu.VMEM((times, AUX_STEP, w, 2 * w), bf),
            pltpu.VMEM((times, AUX_STEP, w, band), bf),
            pltpu.VMEM((2 * times, AUX_STEP, w, 2 * w), bf),
            pltpu.VMEM((2 * times, AUX_STEP, w, w), bf),
            pltpu.VMEM((times, aux, w * band), bf),
            pltpu.VMEM((aux, w * band), bf),
        ],
        compiler_params=pltpu.CompilerParams(vmem_limit_bytes=VMEM_LIMIT),
        cost_estimate=pl.CostEstimate(flops=flops // 50, bytes_accessed=1_000_000, transcendentals=0),
        name="own_terms",
    )(odd, tensor, flag, occ, vir, occ_flag, vir_flag, even_pair, odd_pair)


def hold_kernel(parts, wide_hbm, thin_hbm, wide_ref, thin_ref, sems):
    copies = []
    for n, (source, target) in enumerate(((wide_hbm, wide_ref), (thin_hbm, thin_ref))):
        share = source.shape[2] // parts
        for j in range(parts):
            at = pl.ds(j * share, share)
            copies.append(
                pltpu.make_async_copy(source.at[:, :, at], target.at[:, :, at], sems.at[n, j])
            )
    for copy in copies:
        copy.start()
    for copy in copies:
        copy.wait()


def hold(wide, thin):
    parts = 4
    return pl.pallas_call(
        functools.partial(hold_kernel, parts),
        in_specs=[ANY, ANY],
        out_specs=[pl.BlockSpec(memory_space=pltpu.VMEM)] * 2,
        out_shape=[pltpu.VMEM(wide.shape, wide.dtype), pltpu.VMEM(thin.shape, thin.dtype)],
        scratch_shapes=[pltpu.SemaphoreType.DMA((2, parts))],
        compiler_params=pltpu.CompilerParams(vmem_limit_bytes=NEAR_LIMIT),
        name="hold",
    )(wide, thin)


def in_vmem(value):
    return pltpu.with_memory_space_constraint(value, pltpu.VMEM)


def in_hbm(value):
    return pltpu.with_memory_space_constraint(value, pltpu.HBM)


def near_kernel(begin, steps, earlier, wide, thin, x_hbm, l_hbm, *rest):
    before, rest = rest[:earlier], rest[earlier:]
    out_ref, x, l, total, held, sems, held_sems = rest
    slots, aux, w = wide.shape[0], wide.shape[1], l.shape[3]
    direct = earlier > 0
    times = slots // 2

    def copies(s):
        rows = pl.ds(s * ROW_STEP, ROW_STEP)
        return [
            pltpu.make_async_copy(x_hbm.at[:, rows], x.at[s], sems.at[s, 0]),
            pltpu.make_async_copy(l_hbm.at[:, rows], l.at[s], sems.at[s, 1]),
        ]

    fetch = []
    for n, ref in enumerate(before):
        size = ref.shape[0]
        fetch.append(
            pltpu.make_async_copy(ref, held.at[n, pl.ds(0, size)], held_sems.at[n])
        )
    for s in range(0 if direct else min(AHEAD, steps)):
        for copy in copies(s):
            copy.start()
    for copy in fetch:
        copy.start()
    total[...] = jnp.zeros_like(total)
    for s in range(steps):
        if direct:
            rows = slice(s * ROW_STEP, (s + 1) * ROW_STEP)
            x_s, l_s = x_hbm[:, rows], l_hbm[:, rows]
        else:
            if s + AHEAD < steps:
                for copy in copies(s + AHEAD):
                    copy.start()
            for copy in copies(s):
                copy.wait()
            x_s, l_s = x[s], l[s]
        far = begin + s * ROW_STEP
        wide_s = wide[:, :, far * 2 * w : (far + ROW_STEP) * 2 * w]
        thin_s = thin[:, :, far * w : (far + ROW_STEP) * w]
        total[...] += dot_nt(wide_s.reshape(slots * aux, ROW_STEP * 2 * w), flat(x_s)) + dot_nt(
            thin_s.reshape(slots * aux, ROW_STEP * w), flat(l_s)
        )
    if not earlier:
        out_ref[...] = total[...]
        return
    for copy in fetch:
        copy.wait()
    half = times * aux
    for n in range(1, earlier):
        total[...] += held[n]
    for t in range(times):
        rows = slice(t * aux, (t + 1) * aux)
        out_ref[rows] = held[0, rows] + total[rows] + total[half + t * aux : half + (t + 1) * aux].T


def near_sum(wide, thin, x, l, begin, rows, before=()):
    slots, aux, _ = wide.shape
    w = l.shape[2]
    steps = rows // ROW_STEP
    shape = (slots // 2 * aux if before else slots * aux, aux)
    bf = jnp.bfloat16
    vmem = pl.BlockSpec(memory_space=pltpu.VMEM)
    return pl.pallas_call(
        functools.partial(near_kernel, begin, steps, len(before)),
        in_specs=[vmem, vmem] + [vmem if before else HBM] * 2 + [ANY] * len(before),
        out_specs=vmem,
        out_shape=jax.ShapeDtypeStruct(shape, jnp.float32),
        scratch_shapes=[
            pltpu.VMEM((steps, aux, ROW_STEP, 2 * w), bf),
            pltpu.VMEM((steps, aux, ROW_STEP, w), bf),
            pltpu.VMEM((slots * aux, aux), jnp.float32),
            pltpu.VMEM((max(len(before), 1), slots * aux, aux), jnp.float32),
            pltpu.SemaphoreType.DMA((steps, 2)),
            pltpu.SemaphoreType.DMA((max(len(before), 1),)),
        ],
        compiler_params=pltpu.CompilerParams(vmem_limit_bytes=NEAR_LIMIT),
        cost_estimate=pl.CostEstimate(
            flops=20 * slots * aux * aux * rows * 3 * w,
            bytes_accessed=20 * (slots + 1) * aux * rows * 3 * w,
            transcendentals=0,
        ),
        name="near_sum",
    )(in_vmem(wide), in_vmem(thin), *map(in_vmem if before else in_hbm, (x, l)), *before)


def scattered_sum(value, axis):
    count = lax.axis_size(axis)
    me = lax.axis_index(axis)
    share = value.shape[0] // count
    if count & (count - 1):
        return lax.dynamic_slice_in_dim(lax.psum(value, axis), me * share, share, 0)
    bits = count.bit_length() - 1
    current = value.reshape((2,) * bits + (share, value.shape[1]))
    left = list(range(bits))
    while left:
        chosen = left[-2:]

        def pick(flips):
            block = current
            for bit in chosen:
                dim = len(left) - 1 - left.index(bit)
                at = ((me >> bit) & 1) ^ ((flips >> bit) & 1)
                block = lax.dynamic_slice_in_dim(block, at, 1, dim)
            return block.reshape((2,) * (len(left) - len(chosen)) + (share, value.shape[1]))

        total = pick(0)
        for code in reversed(range(1, 1 << len(chosen))):
            flips = sum(((code >> j) & 1) << bit for j, bit in enumerate(chosen))
            pairs = [(i, i ^ flips) for i in range(count)]
            total = total + lax.ppermute(pick(flips), axis, pairs)
        current = total
        left = left[: len(left) - len(chosen)]
    return current


def body(tensor, tensor_mask, occupied, occupied_mask, virtual, virtual_mask):
    count = lax.axis_size("orb")
    forward = [(i, i + 1) for i in range(count - 1)]
    backward = [(i + 1, i) for i in range(count - 1)]

    odd = (lax.axis_index("orb") & 1).astype(jnp.int32).reshape(1)
    even_pair, odd_pair = edges(odd, occupied, virtual, occupied_mask, virtual_mask)
    source, even_pair, odd_pair = lax.optimization_barrier((tensor, even_pair, odd_pair))
    swaps = [[], []]
    for i, j in forward:
        swaps[i % 2] += [(i, j), (j, i)]
    odd_pair = lax.ppermute(odd_pair, "orb", swaps[1])
    even_pair = lax.ppermute(even_pair, "orb", swaps[0])
    arrived = []
    for begin, rows in CUTS:
        x = cut(source, tensor_mask, (1, 2), begin, rows)
        source, x = lax.optimization_barrier((source, x))
        l = cut(source, tensor_mask, (0,), begin, rows)
        source, x, l, odd_pair, even_pair = lax.optimization_barrier(
            (source, x, l, odd_pair, even_pair)
        )
        arrived.append((lax.ppermute(x, "orb", forward), lax.ppermute(l, "orb", backward)))

    total, wide, thin = own_terms(
        odd, tensor, tensor_mask, occupied, virtual, occupied_mask, virtual_mask, even_pair, odd_pair
    )
    wide, thin = hold(wide, thin)
    before = [total]
    for (begin, rows), (x, l) in zip(CUTS, arrived, strict=True):
        last = len(before) == len(CUTS)
        before.append(near_sum(wide, thin, x, l, begin, rows, before if last else ()))
    return scattered_sum(before[-1], "orb")


def solution(mesh):
    return jax.shard_map(
        body,
        mesh=mesh,
        in_specs=(
            P("grp", "orb", None),
            P("orb", "grp"),
            P("grp", "orb", None),
            P("grp", "orb", None),
            P("grp", "orb", None),
            P("grp", "orb", None),
        ),
        out_specs=P("orb", "grp"),
        check_vma=False,
    )
```

```python
import functools
import math

import jax
import jax.numpy as jnp
from jax import lax
from jax.experimental import pallas as pl
from jax.experimental.pallas import tpu as pltpu
from jax.sharding import PartitionSpec as P

CUTS = ((0, 80), (80, 48))
AUX_STEP = 16
GROUP = 8
ROW_STEP = 16
AHEAD = 2
VMEM_LIMIT = 60 * 1024 * 1024
NEAR_LIMIT = 12 * 1024 * 1024
ANY = pl.BlockSpec(memory_space=pl.ANY)
HBM = pl.BlockSpec(memory_space=pltpu.HBM)
SMEM = pl.BlockSpec(memory_space=pltpu.SMEM)


def dot(lhs, rhs):
    return jnp.dot(lhs, rhs, preferred_element_type=jnp.float32)


def dot_nt(lhs, rhs):
    return lax.dot_general(
        lhs, rhs, (((1,), (1,)), ((), ())), preferred_element_type=jnp.float32
    )


def flat(block):
    return pltpu.einshape("plc->p(lc)", block)


def kept(flag, block):
    return jnp.where(flag != 0, block, jnp.zeros_like(block))


def part(ref, t, k, width, flag):
    return kept(flag[t, 0, k], ref[t, :, k * width : (k + 1) * width])


def edge_kernel(times, width, odd_ref, occ_ref, vir_ref, occ_flag, vir_flag, even_pair, odd_pair):
    w = width

    def put(ref, blocks):
        for t in range(times):
            for n, (source, flag, k) in enumerate(blocks):
                ref[t, :, n * w : (n + 1) * w] = part(source, t, k, w, flag)

    vir, occ = (vir_ref, vir_flag), (occ_ref, occ_flag)
    up = [(*vir, 1), (*vir, 2), (*occ, 2)]
    down = [(*vir, 0), (*vir, 1), (*occ, 0)]

    @pl.when(odd_ref[0] == 0)
    def first_of_pair():
        put(even_pair, up)
        put(odd_pair, down)

    @pl.when(odd_ref[0] != 0)
    def second_of_pair():
        put(even_pair, down)
        put(odd_pair, up)


def edges(odd, occ, vir, occ_flag, vir_flag):
    times, w, _ = occ.shape
    whole = pl.BlockSpec(occ.shape, lambda i: (0, 0, 0))
    return pl.pallas_call(
        functools.partial(edge_kernel, times, w),
        grid=(1,),
        in_specs=[SMEM, whole, whole, SMEM, SMEM],
        out_specs=[whole, whole],
        out_shape=[jax.ShapeDtypeStruct(occ.shape, occ.dtype)] * 2,
        name="edges",
    )(odd, occ, vir, occ_flag, vir_flag)


def cut_kernel(width, b_ref, flag_ref, x_ref, l_ref):
    w = width
    l_ref[...] = kept(flag_ref[0, 0], b_ref[:, :, :w])
    x_ref[:, :, :w] = kept(flag_ref[0, 1], b_ref[:, :, w : 2 * w])
    x_ref[:, :, w:] = kept(flag_ref[0, 2], b_ref[:, :, 2 * w :])


def cut(tensor, flag, begin, rows):
    aux, w, band = tensor.shape
    size = math.gcd(begin, rows)
    step = aux if size <= ROW_STEP else AUX_STEP
    base = begin // size

    def spec(lanes, first):
        return pl.BlockSpec((step, size, lanes), lambda i, j: (i, first + j, 0))

    return pl.pallas_call(
        functools.partial(cut_kernel, w),
        grid=(aux // step, rows // size),
        in_specs=[spec(band, base), SMEM],
        out_specs=[spec(2 * w, 0), spec(w, 0)],
        out_shape=[
            jax.ShapeDtypeStruct((aux, rows, 2 * w), tensor.dtype),
            jax.ShapeDtypeStruct((aux, rows, w), tensor.dtype),
        ],
        compiler_params=pltpu.CompilerParams(vmem_limit_bytes=VMEM_LIMIT),
        name="cut",
    )(tensor, flag)


def own_kernel(
    times, width, odd_ref, b_ref, flag_ref, occ_ref, vir_ref, occ_flag, vir_flag, even_pair, odd_pair,
    sum_ref, wide_ref, thin_ref,
    left_w, right_w, low_w, occ_w, masked, u, x, left, own_n, wide_n, thin_n, flat_own, flat_b,
):
    w = width
    step = pl.program_id(0)

    @pl.when(step == 0)
    def build():
        for t in range(times):
            v_low, v_own, v_high = (part(vir_ref, t, k, w, vir_flag) for k in range(3))
            o_low, o_own, o_high = (part(occ_ref, t, k, w, occ_flag) for k in range(3))
            from_even = [even_pair[t, :, k * w : (k + 1) * w] for k in range(3)]
            from_odd = [odd_pair[t, :, k * w : (k + 1) * w] for k in range(3)]
            odd = odd_ref[0] != 0
            below_own, below_up, below_occ = (
                jnp.where(odd, one, two) for one, two in zip(from_even, from_odd, strict=True)
            )
            above_down, above_own, above_occ = (
                jnp.where(odd, two, one) for one, two in zip(from_even, from_odd, strict=True)
            )

            def cols(slot):
                return slice((slot * times + t) * w, (slot * times + t + 1) * w)

            left_w[:, cols(0)] = v_low.T
            left_w[:, cols(1)] = below_up
            right_w[:w, cols(0)] = v_own.T
            right_w[w:, cols(0)] = v_high.T
            right_w[:w, cols(1)] = v_own
            right_w[w:, cols(1)] = above_down
            right_w[:w, cols(2)] = above_down.T
            right_w[w:, cols(2)] = above_own.T
            low_w[:w, cols(0)] = below_own.T
            low_w[w:, cols(0)] = below_up.T
            low_w[:w, cols(1)] = below_own
            low_w[w:, cols(1)] = v_low

            occ_w[t, 0] = o_own
            occ_w[t, 1] = below_occ
            occ_w[t, 2] = o_low.T
            occ_w[t, 3] = above_occ
            occ_w[t, 4] = o_high.T

    bf = jnp.bfloat16
    for k in range(3):
        block = slice(k * w, (k + 1) * w)
        masked[:, :, block] = kept(flag_ref[0, k], b_ref[:, :, block])

    loops = AUX_STEP // GROUP
    rows = w // loops
    here = pl.ds(pl.multiple_of(step * AUX_STEP, AUX_STEP), AUX_STEP)

    def lay(g, source, target):
        first = pl.multiple_of(g * rows, rows)
        length = rows * source.shape[2]
        at = pl.ds(pl.multiple_of(g * length, length), length)
        target(at, flat(source[:, pl.ds(first, rows), :]))

    def to_own(t):
        def store(at, value):
            flat_own[t, here, at] = value

        return store

    def to_b(at, value):
        flat_b[here, at] = value

    def to_out(ref, slot):
        def store(at, value):
            ref[slot, :, at] = value

        return store

    def virtual_phase(g):
        group = pl.ds(g * GROUP, GROUP)
        lhs = masked[group].reshape(GROUP * w, 3 * w)
        from_left = dot(lhs[:, :w], left_w[...])
        from_right = dot(lhs[:, w:], right_w[...])
        from_low = dot(lhs[:, : 2 * w], low_w[...])

        def piece(product, slot, t):
            return product[:, (slot * times + t) * w : (slot * times + t + 1) * w]

        def put(ref, t, lanes, value):
            ref[t, group, :, lanes] = value.astype(bf).reshape(GROUP, w, w)

        one, two, three = slice(None, w), slice(w, 2 * w), slice(2 * w, None)
        for t in range(times):
            left_c, left_b = piece(from_left, 0, t), piece(from_left, 1, t)
            put(u, t, one, piece(from_low, 0, t))
            put(u, t, two, piece(from_right, 0, t) + left_c)
            put(u, t, three, piece(from_right, 2, t))
            put(x, t, one, piece(from_low, 1, t))
            put(x, t, two, piece(from_right, 1, t) + left_b)
            put(left, t, one, left_c)
            put(left, t, two, left_b)

    def pairs(g):
        return [(g * GROUP + j, g * GROUP + j + 1) for j in range(0, GROUP, 2)]

    def in_pair(occ, source, lanes, target, lanes_to, p, q):
        both = dot(occ, jnp.concatenate([source[p, :, lanes], source[q, :, lanes]], axis=1))
        both = both.astype(bf)
        target[p, :, lanes_to] = both[:, :w]
        target[q, :, lanes_to] = both[:, w:]

    def own_phase(t, g):
        occ = occ_w[t, 0:2].reshape(2 * w, w)
        for j in range(GROUP):
            p = g * GROUP + j
            both = dot(occ, u[t, p, :, : 2 * w]).astype(bf)
            own_n[t, p, :, : 2 * w] = both[:w]
            wide_n[t, p] = both[w:]
        last = slice(2 * w, 3 * w)
        for p, q in pairs(g):
            in_pair(occ_w[t, 0], u.at[t], last, own_n.at[t], last, p, q)

    def other_phase(t, g):
        for j in range(GROUP):
            p = g * GROUP + j
            wide_n[times + t, p] = dot(occ_w[t, 2], x[t, p]).astype(bf)
        for p, q in pairs(g):
            every = slice(None)
            in_pair(occ_w[t, 3], left.at[t], slice(None, w), thin_n.at[t], every, p, q)
            in_pair(occ_w[t, 4], left.at[t], slice(w, None), thin_n.at[times + t], every, p, q)

    def lay_b(g):
        lay(g, masked, to_b)

    def lay_own(t, g):
        lay(g, own_n.at[t], to_own(t))
        lay(g, wide_n.at[t], to_out(wide_ref, t))

    def lay_other(t, g):
        lay(g, wide_n.at[times + t], to_out(wide_ref, times + t))
        lay(g, thin_n.at[t], to_out(thin_ref, t))
        lay(g, thin_n.at[times + t], to_out(thin_ref, times + t))

    work, laying = [virtual_phase], [lay_b]
    for t in range(times):
        work += [functools.partial(own_phase, t), functools.partial(other_phase, t)]
        laying += [functools.partial(lay_own, t), functools.partial(lay_other, t)]
    for n, phase in enumerate(work):

        def both(g, phase=phase, before=laying[n - 1] if n else None):
            phase(g)
            if before is not None:
                before(g)

        for g in range(loops):
            both(g)
    for g in range(loops):
        laying[-1](g)

    @pl.when(step == pl.num_programs(0) - 1)
    def add_up():
        count = times * flat_own.shape[1]
        length = flat_own.shape[2]
        share = length // 8
        total = None
        for n in range(8):
            at = slice(n * share, (n + 1) * share)
            term = dot_nt(flat_own[:, :, at].reshape(count, share), flat_b[:, at])
            total = term if total is None else total + term
        sum_ref[...] = total


def own_terms(odd, tensor, flag, occ, vir, occ_flag, vir_flag, even_pair, odd_pair):
    aux, w, band = tensor.shape
    times = occ.shape[0]
    bf = jnp.bfloat16
    whole = pl.BlockSpec(occ.shape, lambda i: (0, 0, 0))

    flops = 2 * aux * w * w * w * (14 * times + 9 * times)
    return pl.pallas_call(
        functools.partial(own_kernel, times, w),
        grid=(aux // AUX_STEP,),
        in_specs=[
            SMEM,
            pl.BlockSpec((AUX_STEP, w, band), lambda i: (i, 0, 0)),
            SMEM, whole, whole, SMEM, SMEM, whole, whole,
        ],
        out_specs=[
            pl.BlockSpec((times * aux, aux), lambda i: (0, 0)),
            pl.BlockSpec((2 * times, AUX_STEP, 2 * w * w), lambda i: (0, i, 0)),
            pl.BlockSpec((2 * times, AUX_STEP, w * w), lambda i: (0, i, 0)),
        ],
        out_shape=[
            jax.ShapeDtypeStruct((times * aux, aux), jnp.float32),
            jax.ShapeDtypeStruct((2 * times, aux, 2 * w * w), bf),
            jax.ShapeDtypeStruct((2 * times, aux, w * w), bf),
        ],
        scratch_shapes=[
            pltpu.VMEM((w, 2 * times * w), bf),
            pltpu.VMEM((2 * w, 3 * times * w), bf),
            pltpu.VMEM((2 * w, 2 * times * w), bf),
            pltpu.VMEM((times, 5, w, w), bf),
            pltpu.VMEM((AUX_STEP, w, band), bf),
            pltpu.VMEM((times, AUX_STEP, w, band), bf),
            pltpu.VMEM((times, AUX_STEP, w, 2 * w), bf),
            pltpu.VMEM((times, AUX_STEP, w, 2 * w), bf),
            pltpu.VMEM((times, AUX_STEP, w, band), bf),
            pltpu.VMEM((2 * times, AUX_STEP, w, 2 * w), bf),
            pltpu.VMEM((2 * times, AUX_STEP, w, w), bf),
            pltpu.VMEM((times, aux, w * band), bf),
            pltpu.VMEM((aux, w * band), bf),
        ],
        compiler_params=pltpu.CompilerParams(vmem_limit_bytes=VMEM_LIMIT),
        cost_estimate=pl.CostEstimate(flops=flops // 50, bytes_accessed=1_000_000, transcendentals=0),
        name="own_terms",
    )(odd, tensor, flag, occ, vir, occ_flag, vir_flag, even_pair, odd_pair)


def hold_kernel(parts, wide_hbm, thin_hbm, wide_ref, thin_ref, sems):
    copies = []
    for n, (source, target) in enumerate(((wide_hbm, wide_ref), (thin_hbm, thin_ref))):
        share = source.shape[2] // parts
        for j in range(parts):
            at = pl.ds(j * share, share)
            copies.append(
                pltpu.make_async_copy(source.at[:, :, at], target.at[:, :, at], sems.at[n, j])
            )
    for copy in copies:
        copy.start()
    for copy in copies:
        copy.wait()


def hold(wide, thin):
    parts = 4
    return pl.pallas_call(
        functools.partial(hold_kernel, parts),
        in_specs=[ANY, ANY],
        out_specs=[pl.BlockSpec(memory_space=pltpu.VMEM)] * 2,
        out_shape=[pltpu.VMEM(wide.shape, wide.dtype), pltpu.VMEM(thin.shape, thin.dtype)],
        scratch_shapes=[pltpu.SemaphoreType.DMA((2, parts))],
        compiler_params=pltpu.CompilerParams(vmem_limit_bytes=NEAR_LIMIT),
        name="hold",
    )(wide, thin)


def in_vmem(value):
    return pltpu.with_memory_space_constraint(value, pltpu.VMEM)


def in_hbm(value):
    return pltpu.with_memory_space_constraint(value, pltpu.HBM)


def near_kernel(begin, steps, earlier, wide, thin, x_hbm, l_hbm, *rest):
    before, rest = rest[:earlier], rest[earlier:]
    out_ref, x, l, total, held, sems, held_sems = rest
    slots, aux, w = wide.shape[0], wide.shape[1], l.shape[3]
    direct = earlier > 0
    times = slots // 2

    def copies(s):
        rows = pl.ds(s * ROW_STEP, ROW_STEP)
        return [
            pltpu.make_async_copy(x_hbm.at[:, rows], x.at[s], sems.at[s, 0]),
            pltpu.make_async_copy(l_hbm.at[:, rows], l.at[s], sems.at[s, 1]),
        ]

    fetch = []
    for n, ref in enumerate(before):
        size = ref.shape[0]
        fetch.append(
            pltpu.make_async_copy(ref, held.at[n, pl.ds(0, size)], held_sems.at[n])
        )
    for s in range(0 if direct else min(AHEAD, steps)):
        for copy in copies(s):
            copy.start()
    for copy in fetch:
        copy.start()
    total[...] = jnp.zeros_like(total)
    for s in range(steps):
        if direct:
            rows = slice(s * ROW_STEP, (s + 1) * ROW_STEP)
            x_s, l_s = x_hbm[:, rows], l_hbm[:, rows]
        else:
            if s + AHEAD < steps:
                for copy in copies(s + AHEAD):
                    copy.start()
            for copy in copies(s):
                copy.wait()
            x_s, l_s = x[s], l[s]
        far = begin + s * ROW_STEP
        wide_s = wide[:, :, far * 2 * w : (far + ROW_STEP) * 2 * w]
        thin_s = thin[:, :, far * w : (far + ROW_STEP) * w]
        total[...] += dot_nt(wide_s.reshape(slots * aux, ROW_STEP * 2 * w), flat(x_s)) + dot_nt(
            thin_s.reshape(slots * aux, ROW_STEP * w), flat(l_s)
        )
    if not earlier:
        out_ref[...] = total[...]
        return
    for copy in fetch:
        copy.wait()
    half = times * aux
    for n in range(1, earlier):
        total[...] += held[n]
    for t in range(times):
        rows = slice(t * aux, (t + 1) * aux)
        out_ref[rows] = held[0, rows] + total[rows] + total[half + t * aux : half + (t + 1) * aux].T


def near_sum(wide, thin, x, l, begin, rows, before=()):
    slots, aux, _ = wide.shape
    w = l.shape[2]
    steps = rows // ROW_STEP
    shape = (slots // 2 * aux if before else slots * aux, aux)
    bf = jnp.bfloat16
    vmem = pl.BlockSpec(memory_space=pltpu.VMEM)
    return pl.pallas_call(
        functools.partial(near_kernel, begin, steps, len(before)),
        in_specs=[vmem, vmem] + [vmem if before else HBM] * 2 + [ANY] * len(before),
        out_specs=vmem,
        out_shape=jax.ShapeDtypeStruct(shape, jnp.float32),
        scratch_shapes=[
            pltpu.VMEM((steps, aux, ROW_STEP, 2 * w), bf),
            pltpu.VMEM((steps, aux, ROW_STEP, w), bf),
            pltpu.VMEM((slots * aux, aux), jnp.float32),
            pltpu.VMEM((max(len(before), 1), slots * aux, aux), jnp.float32),
            pltpu.SemaphoreType.DMA((steps, 2)),
            pltpu.SemaphoreType.DMA((max(len(before), 1),)),
        ],
        compiler_params=pltpu.CompilerParams(vmem_limit_bytes=NEAR_LIMIT),
        cost_estimate=pl.CostEstimate(
            flops=20 * slots * aux * aux * rows * 3 * w,
            bytes_accessed=20 * (slots + 1) * aux * rows * 3 * w,
            transcendentals=0,
        ),
        name="near_sum",
    )(in_vmem(wide), in_vmem(thin), *map(in_vmem if before else in_hbm, (x, l)), *before)


def scattered_sum(value, axis):
    count = lax.axis_size(axis)
    me = lax.axis_index(axis)
    share = value.shape[0] // count
    if count & (count - 1):
        return lax.dynamic_slice_in_dim(lax.psum(value, axis), me * share, share, 0)
    bits = count.bit_length() - 1
    current = value.reshape((2,) * bits + (share, value.shape[1]))
    left = list(range(bits))
    while left:
        chosen = left[-2:]

        def pick(flips):
            block = current
            for bit in chosen:
                dim = len(left) - 1 - left.index(bit)
                at = ((me >> bit) & 1) ^ ((flips >> bit) & 1)
                block = lax.dynamic_slice_in_dim(block, at, 1, dim)
            return block.reshape((2,) * (len(left) - len(chosen)) + (share, value.shape[1]))

        total = pick(0)
        for code in reversed(range(1, 1 << len(chosen))):
            flips = sum(((code >> j) & 1) << bit for j, bit in enumerate(chosen))
            pairs = [(i, i ^ flips) for i in range(count)]
            total = total + lax.ppermute(pick(flips), axis, pairs)
        current = total
        left = left[: len(left) - len(chosen)]
    return current


def body(tensor, tensor_mask, occupied, occupied_mask, virtual, virtual_mask):
    count = lax.axis_size("orb")
    forward = [(i, i + 1) for i in range(count - 1)]
    backward = [(i + 1, i) for i in range(count - 1)]

    odd = (lax.axis_index("orb") & 1).astype(jnp.int32).reshape(1)
    even_pair, odd_pair = edges(odd, occupied, virtual, occupied_mask, virtual_mask)
    source, even_pair, odd_pair = lax.optimization_barrier((tensor, even_pair, odd_pair))
    swaps = [[], []]
    for i, j in forward:
        swaps[i % 2] += [(i, j), (j, i)]
    odd_pair = lax.ppermute(odd_pair, "orb", swaps[1])
    even_pair = lax.ppermute(even_pair, "orb", swaps[0])
    arrived = []
    for begin, rows in CUTS:
        x, l = cut(source, tensor_mask, begin, rows)
        source, x, l, odd_pair, even_pair = lax.optimization_barrier(
            (source, x, l, odd_pair, even_pair)
        )
        arrived.append((lax.ppermute(x, "orb", forward), lax.ppermute(l, "orb", backward)))

    total, wide, thin = own_terms(
        odd, tensor, tensor_mask, occupied, virtual, occupied_mask, virtual_mask, even_pair, odd_pair
    )
    wide, thin = hold(wide, thin)
    before = [total]
    for (begin, rows), (x, l) in zip(CUTS, arrived, strict=True):
        last = len(before) == len(CUTS)
        before.append(near_sum(wide, thin, x, l, begin, rows, before if last else ()))
    return scattered_sum(before[-1], "orb")


def solution(mesh):
    return jax.shard_map(
        body,
        mesh=mesh,
        in_specs=(
            P("grp", "orb", None),
            P("orb", "grp"),
            P("grp", "orb", None),
            P("grp", "orb", None),
            P("grp", "orb", None),
            P("grp", "orb", None),
        ),
        out_specs=P("orb", "grp"),
        check_vma=False,
    )
```

```python
import functools
import math

import jax
import jax.numpy as jnp
from jax import lax
from jax.experimental import pallas as pl
from jax.experimental.pallas import tpu as pltpu
from jax.sharding import PartitionSpec as P

CUTS = ((0, 80), (80, 48))
AUX_STEP = 16
GROUP = 8
ROW_STEP = 16
AHEAD = 2
VMEM_LIMIT = 60 * 1024 * 1024
NEAR_LIMIT = 12 * 1024 * 1024
ANY = pl.BlockSpec(memory_space=pl.ANY)
HBM = pl.BlockSpec(memory_space=pltpu.HBM)
SMEM = pl.BlockSpec(memory_space=pltpu.SMEM)


def dot(lhs, rhs):
    return jnp.dot(lhs, rhs, preferred_element_type=jnp.float32)


def dot_nt(lhs, rhs):
    return lax.dot_general(
        lhs, rhs, (((1,), (1,)), ((), ())), preferred_element_type=jnp.float32
    )


def flat(block):
    return pltpu.einshape("plc->p(lc)", block)


def kept(flag, block):
    return jnp.where(flag != 0, block, jnp.zeros_like(block))


def part(ref, t, k, width, flag):
    return kept(flag[t, 0, k], ref[t, :, k * width : (k + 1) * width])


def edge_kernel(times, width, odd_ref, occ_ref, vir_ref, occ_flag, vir_flag, even_pair, odd_pair):
    w = width

    def put(ref, blocks):
        for t in range(times):
            for n, (source, flag, k) in enumerate(blocks):
                ref[t, :, n * w : (n + 1) * w] = part(source, t, k, w, flag)

    vir, occ = (vir_ref, vir_flag), (occ_ref, occ_flag)
    up = [(*vir, 1), (*vir, 2), (*occ, 2)]
    down = [(*vir, 0), (*vir, 1), (*occ, 0)]

    @pl.when(odd_ref[0] == 0)
    def first_of_pair():
        put(even_pair, up)
        put(odd_pair, down)

    @pl.when(odd_ref[0] != 0)
    def second_of_pair():
        put(even_pair, down)
        put(odd_pair, up)


def edges(odd, occ, vir, occ_flag, vir_flag):
    times, w, _ = occ.shape
    whole = pl.BlockSpec(occ.shape, lambda i: (0, 0, 0))
    return pl.pallas_call(
        functools.partial(edge_kernel, times, w),
        grid=(1,),
        in_specs=[SMEM, whole, whole, SMEM, SMEM],
        out_specs=[whole, whole],
        out_shape=[jax.ShapeDtypeStruct(occ.shape, occ.dtype)] * 2,
        name="edges",
    )(odd, occ, vir, occ_flag, vir_flag)


def cut_kernel(width, b_ref, flag_ref, x_ref, l_ref):
    w = width
    l_ref[...] = kept(flag_ref[0, 0], b_ref[:, :, :w])
    x_ref[:, :, :w] = kept(flag_ref[0, 1], b_ref[:, :, w : 2 * w])
    x_ref[:, :, w:] = kept(flag_ref[0, 2], b_ref[:, :, 2 * w :])


def cut(tensor, flag, begin, rows):
    aux, w, band = tensor.shape
    size = math.gcd(begin, rows)
    step = aux if size <= ROW_STEP else AUX_STEP
    base = begin // size

    def spec(lanes, first):
        return pl.BlockSpec((step, size, lanes), lambda i, j: (i, first + j, 0))

    return pl.pallas_call(
        functools.partial(cut_kernel, w),
        grid=(aux // step, rows // size),
        in_specs=[spec(band, base), SMEM],
        out_specs=[spec(2 * w, 0), spec(w, 0)],
        out_shape=[
            jax.ShapeDtypeStruct((aux, rows, 2 * w), tensor.dtype),
            jax.ShapeDtypeStruct((aux, rows, w), tensor.dtype),
        ],
        compiler_params=pltpu.CompilerParams(vmem_limit_bytes=VMEM_LIMIT),
        name="cut",
    )(tensor, flag)


def own_kernel(
    times, width, odd_ref, b_ref, flag_ref, occ_ref, vir_ref, occ_flag, vir_flag, even_pair, odd_pair,
    sum_ref, wide_ref, thin_ref,
    left_w, right_w, low_w, occ_w, masked, u, x, left, own_n, wide_n, thin_n, flat_own, flat_b,
):
    w = width
    step = pl.program_id(0)

    @pl.when(step == 0)
    def build():
        for t in range(times):
            v_low, v_own, v_high = (part(vir_ref, t, k, w, vir_flag) for k in range(3))
            o_low, o_own, o_high = (part(occ_ref, t, k, w, occ_flag) for k in range(3))
            from_even = [even_pair[t, :, k * w : (k + 1) * w] for k in range(3)]
            from_odd = [odd_pair[t, :, k * w : (k + 1) * w] for k in range(3)]
            odd = odd_ref[0] != 0
            below_own, below_up, below_occ = (
                jnp.where(odd, one, two) for one, two in zip(from_even, from_odd, strict=True)
            )
            above_down, above_own, above_occ = (
                jnp.where(odd, two, one) for one, two in zip(from_even, from_odd, strict=True)
            )

            def cols(slot):
                return slice((slot * times + t) * w, (slot * times + t + 1) * w)

            left_w[:, cols(0)] = v_low.T
            left_w[:, cols(1)] = below_up
            right_w[:w, cols(0)] = v_own.T
            right_w[w:, cols(0)] = v_high.T
            right_w[:w, cols(1)] = v_own
            right_w[w:, cols(1)] = above_down
            right_w[:w, cols(2)] = above_down.T
            right_w[w:, cols(2)] = above_own.T
            low_w[:w, cols(0)] = below_own.T
            low_w[w:, cols(0)] = below_up.T
            low_w[:w, cols(1)] = below_own
            low_w[w:, cols(1)] = v_low

            occ_w[t, 0] = o_own
            occ_w[t, 1] = below_occ
            occ_w[t, 2] = o_low.T
            occ_w[t, 3] = above_occ
            occ_w[t, 4] = o_high.T

    bf = jnp.bfloat16
    for k in range(3):
        block = slice(k * w, (k + 1) * w)
        masked[:, :, block] = kept(flag_ref[0, k], b_ref[:, :, block])

    loops = AUX_STEP // GROUP
    rows = w // loops
    here = pl.ds(pl.multiple_of(step * AUX_STEP, AUX_STEP), AUX_STEP)

    def lay(g, source, target):
        first = pl.multiple_of(g * rows, rows)
        length = rows * source.shape[2]
        at = pl.ds(pl.multiple_of(g * length, length), length)
        target(at, flat(source[:, pl.ds(first, rows), :]))

    def to_own(t):
        def store(at, value):
            flat_own[t, here, at] = value

        return store

    def to_b(at, value):
        flat_b[here, at] = value

    def to_out(ref, slot):
        def store(at, value):
            ref[slot, :, at] = value

        return store

    def virtual_phase(g):
        group = pl.ds(g * GROUP, GROUP)
        lhs = masked[group].reshape(GROUP * w, 3 * w)
        from_left = dot(lhs[:, :w], left_w[...])
        from_right = dot(lhs[:, w:], right_w[...])
        from_low = dot(lhs[:, : 2 * w], low_w[...])

        def piece(product, slot, t):
            return product[:, (slot * times + t) * w : (slot * times + t + 1) * w]

        def put(ref, t, lanes, value):
            ref[t, group, :, lanes] = value.astype(bf).reshape(GROUP, w, w)

        one, two, three = slice(None, w), slice(w, 2 * w), slice(2 * w, None)
        for t in range(times):
            left_c, left_b = piece(from_left, 0, t), piece(from_left, 1, t)
            put(u, t, one, piece(from_low, 0, t))
            put(u, t, two, piece(from_right, 0, t) + left_c)
            put(u, t, three, piece(from_right, 2, t))
            put(x, t, one, piece(from_low, 1, t))
            put(x, t, two, piece(from_right, 1, t) + left_b)
            put(left, t, one, left_c)
            put(left, t, two, left_b)

    def pairs(g):
        return [(g * GROUP + j, g * GROUP + j + 1) for j in range(0, GROUP, 2)]

    def in_pair(occ, source, lanes, target, lanes_to, p, q):
        both = dot(occ, jnp.concatenate([source[p, :, lanes], source[q, :, lanes]], axis=1))
        both = both.astype(bf)
        target[p, :, lanes_to] = both[:, :w]
        target[q, :, lanes_to] = both[:, w:]

    def own_phase(t, g):
        occ = occ_w[t, 0:2].reshape(2 * w, w)
        for j in range(GROUP):
            p = g * GROUP + j
            both = dot(occ, u[t, p, :, : 2 * w]).astype(bf)
            own_n[t, p, :, : 2 * w] = both[:w]
            wide_n[t, p] = both[w:]
        last = slice(2 * w, 3 * w)
        for p, q in pairs(g):
            in_pair(occ_w[t, 0], u.at[t], last, own_n.at[t], last, p, q)

    def other_phase(t, g):
        for j in range(GROUP):
            p = g * GROUP + j
            wide_n[times + t, p] = dot(occ_w[t, 2], x[t, p]).astype(bf)
        for p, q in pairs(g):
            every = slice(None)
            in_pair(occ_w[t, 3], left.at[t], slice(None, w), thin_n.at[t], every, p, q)
            in_pair(occ_w[t, 4], left.at[t], slice(w, None), thin_n.at[times + t], every, p, q)

    def lay_b(g):
        lay(g, masked, to_b)

    def lay_own(t, g):
        lay(g, own_n.at[t], to_own(t))
        lay(g, wide_n.at[t], to_out(wide_ref, t))

    def lay_other(t, g):
        lay(g, wide_n.at[times + t], to_out(wide_ref, times + t))
        lay(g, thin_n.at[t], to_out(thin_ref, t))
        lay(g, thin_n.at[times + t], to_out(thin_ref, times + t))

    work, laying = [virtual_phase], [lay_b]
    for t in range(times):
        work += [functools.partial(own_phase, t), functools.partial(other_phase, t)]
        laying += [functools.partial(lay_own, t), functools.partial(lay_other, t)]
    for n, phase in enumerate(work):

        def both(g, phase=phase, before=laying[n - 1] if n else None):
            phase(g)
            if before is not None:
                before(g)

        for g in range(loops):
            both(g)
    for g in range(loops):
        laying[-1](g)

    @pl.when(step == pl.num_programs(0) - 1)
    def add_up():
        count = times * flat_own.shape[1]
        length = flat_own.shape[2]
        share = length // 8
        total = None
        for n in range(8):
            at = slice(n * share, (n + 1) * share)
            term = dot_nt(flat_own[:, :, at].reshape(count, share), flat_b[:, at])
            total = term if total is None else total + term
        sum_ref[...] = total


def own_terms(odd, tensor, flag, occ, vir, occ_flag, vir_flag, even_pair, odd_pair):
    aux, w, band = tensor.shape
    times = occ.shape[0]
    bf = jnp.bfloat16
    whole = pl.BlockSpec(occ.shape, lambda i: (0, 0, 0))

    flops = 2 * aux * w * w * w * (14 * times + 9 * times)
    return pl.pallas_call(
        functools.partial(own_kernel, times, w),
        grid=(aux // AUX_STEP,),
        in_specs=[
            SMEM,
            pl.BlockSpec((AUX_STEP, w, band), lambda i: (i, 0, 0)),
            SMEM, whole, whole, SMEM, SMEM, whole, whole,
        ],
        out_specs=[
            pl.BlockSpec((times * aux, aux), lambda i: (0, 0)),
            pl.BlockSpec((2 * times, AUX_STEP, 2 * w * w), lambda i: (0, i, 0)),
            pl.BlockSpec((2 * times, AUX_STEP, w * w), lambda i: (0, i, 0)),
        ],
        out_shape=[
            jax.ShapeDtypeStruct((times * aux, aux), jnp.float32),
            jax.ShapeDtypeStruct((2 * times, aux, 2 * w * w), bf),
            jax.ShapeDtypeStruct((2 * times, aux, w * w), bf),
        ],
        scratch_shapes=[
            pltpu.VMEM((w, 2 * times * w), bf),
            pltpu.VMEM((2 * w, 3 * times * w), bf),
            pltpu.VMEM((2 * w, 2 * times * w), bf),
            pltpu.VMEM((times, 5, w, w), bf),
            pltpu.VMEM((AUX_STEP, w, band), bf),
            pltpu.VMEM((times, AUX_STEP, w, band), bf),
            pltpu.VMEM((times, AUX_STEP, w, 2 * w), bf),
            pltpu.VMEM((times, AUX_STEP, w, 2 * w), bf),
            pltpu.VMEM((times, AUX_STEP, w, band), bf),
            pltpu.VMEM((2 * times, AUX_STEP, w, 2 * w), bf),
            pltpu.VMEM((2 * times, AUX_STEP, w, w), bf),
            pltpu.VMEM((times, aux, w * band), bf),
            pltpu.VMEM((aux, w * band), bf),
        ],
        compiler_params=pltpu.CompilerParams(vmem_limit_bytes=VMEM_LIMIT),
        cost_estimate=pl.CostEstimate(flops=flops // 50, bytes_accessed=1_000_000, transcendentals=0),
        name="own_terms",
    )(odd, tensor, flag, occ, vir, occ_flag, vir_flag, even_pair, odd_pair)


def hold_kernel(parts, wide_hbm, thin_hbm, wide_ref, thin_ref, sems):
    copies = []
    for n, (source, target) in enumerate(((wide_hbm, wide_ref), (thin_hbm, thin_ref))):
        share = source.shape[2] // parts
        for j in range(parts):
            at = pl.ds(j * share, share)
            copies.append(
                pltpu.make_async_copy(source.at[:, :, at], target.at[:, :, at], sems.at[n, j])
            )
    for copy in copies:
        copy.start()
    for copy in copies:
        copy.wait()


def hold(wide, thin):
    parts = 4
    return pl.pallas_call(
        functools.partial(hold_kernel, parts),
        in_specs=[ANY, ANY],
        out_specs=[pl.BlockSpec(memory_space=pltpu.VMEM)] * 2,
        out_shape=[pltpu.VMEM(wide.shape, wide.dtype), pltpu.VMEM(thin.shape, thin.dtype)],
        scratch_shapes=[pltpu.SemaphoreType.DMA((2, parts))],
        compiler_params=pltpu.CompilerParams(vmem_limit_bytes=NEAR_LIMIT),
        name="hold",
    )(wide, thin)


def in_vmem(value):
    return pltpu.with_memory_space_constraint(value, pltpu.VMEM)


def in_hbm(value):
    return pltpu.with_memory_space_constraint(value, pltpu.HBM)


def near_kernel(begin, steps, earlier, wide, thin, x_hbm, l_hbm, *rest):
    before, rest = rest[:earlier], rest[earlier:]
    out_ref, x, l, total, held, sems, held_sems = rest
    slots, aux, w = wide.shape[0], wide.shape[1], l.shape[3]
    direct = earlier > 0
    times = slots // 2

    def copies(s):
        rows = pl.ds(s * ROW_STEP, ROW_STEP)
        return [
            pltpu.make_async_copy(x_hbm.at[:, rows], x.at[s], sems.at[s, 0]),
            pltpu.make_async_copy(l_hbm.at[:, rows], l.at[s], sems.at[s, 1]),
        ]

    fetch = []
    for n, ref in enumerate(before):
        size = ref.shape[0]
        fetch.append(
            pltpu.make_async_copy(ref, held.at[n, pl.ds(0, size)], held_sems.at[n])
        )
    for s in range(0 if direct else min(AHEAD, steps)):
        for copy in copies(s):
            copy.start()
    for copy in fetch:
        copy.start()
    total[...] = jnp.zeros_like(total)
    for s in range(steps):
        if direct:
            rows = slice(s * ROW_STEP, (s + 1) * ROW_STEP)
            x_s, l_s = x_hbm[:, rows], l_hbm[:, rows]
        else:
            if s + AHEAD < steps:
                for copy in copies(s + AHEAD):
                    copy.start()
            for copy in copies(s):
                copy.wait()
            x_s, l_s = x[s], l[s]
        far = begin + s * ROW_STEP
        wide_s = wide[:, :, far * 2 * w : (far + ROW_STEP) * 2 * w]
        thin_s = thin[:, :, far * w : (far + ROW_STEP) * w]
        total[...] += dot_nt(wide_s.reshape(slots * aux, ROW_STEP * 2 * w), flat(x_s)) + dot_nt(
            thin_s.reshape(slots * aux, ROW_STEP * w), flat(l_s)
        )
    if not earlier:
        out_ref[...] = total[...]
        return
    for copy in fetch:
        copy.wait()
    half = times * aux
    for n in range(1, earlier):
        total[...] += held[n]
    for t in range(times):
        rows = slice(t * aux, (t + 1) * aux)
        out_ref[rows] = held[0, rows] + total[rows] + total[half + t * aux : half + (t + 1) * aux].T


def near_sum(wide, thin, x, l, begin, rows, before=()):
    slots, aux, _ = wide.shape
    w = l.shape[2]
    steps = rows // ROW_STEP
    shape = (slots // 2 * aux if before else slots * aux, aux)
    bf = jnp.bfloat16
    vmem = pl.BlockSpec(memory_space=pltpu.VMEM)
    return pl.pallas_call(
        functools.partial(near_kernel, begin, steps, len(before)),
        in_specs=[vmem, vmem] + [vmem if before else HBM] * 2 + [ANY] * len(before),
        out_specs=vmem,
        out_shape=jax.ShapeDtypeStruct(shape, jnp.float32),
        scratch_shapes=[
            pltpu.VMEM((steps, aux, ROW_STEP, 2 * w), bf),
            pltpu.VMEM((steps, aux, ROW_STEP, w), bf),
            pltpu.VMEM((slots * aux, aux), jnp.float32),
            pltpu.VMEM((max(len(before), 1), slots * aux, aux), jnp.float32),
            pltpu.SemaphoreType.DMA((steps, 2)),
            pltpu.SemaphoreType.DMA((max(len(before), 1),)),
        ],
        compiler_params=pltpu.CompilerParams(vmem_limit_bytes=NEAR_LIMIT),
        cost_estimate=pl.CostEstimate(
            flops=20 * slots * aux * aux * rows * 3 * w,
            bytes_accessed=20 * (slots + 1) * aux * rows * 3 * w,
            transcendentals=0,
        ),
        name="near_sum",
    )(in_vmem(wide), in_vmem(thin), *map(in_vmem if before else in_hbm, (x, l)), *before)


def scattered_sum(value, axis):
    count = lax.axis_size(axis)
    me = lax.axis_index(axis)
    share = value.shape[0] // count
    if count & (count - 1):
        return lax.dynamic_slice_in_dim(lax.psum(value, axis), me * share, share, 0)
    bits = count.bit_length() - 1
    current = value.reshape((2,) * bits + (share, value.shape[1]))
    left = list(range(bits))
    while left:
        chosen = left[-2:]

        def pick(flips):
            block = current
            for bit in chosen:
                dim = len(left) - 1 - left.index(bit)
                at = ((me >> bit) & 1) ^ ((flips >> bit) & 1)
                block = lax.dynamic_slice_in_dim(block, at, 1, dim)
            return block.reshape((2,) * (len(left) - len(chosen)) + (share, value.shape[1]))

        total = pick(0)
        codes = list(reversed(range(1, 1 << len(chosen))))
        if len(left) < bits:
            codes = codes[-1:] + codes[:-1]
        for code in codes:
            flips = sum(((code >> j) & 1) << bit for j, bit in enumerate(chosen))
            pairs = [(i, i ^ flips) for i in range(count)]
            total = total + lax.ppermute(pick(flips), axis, pairs)
        current = total
        left = left[: len(left) - len(chosen)]
    return current


def body(tensor, tensor_mask, occupied, occupied_mask, virtual, virtual_mask):
    count = lax.axis_size("orb")
    forward = [(i, i + 1) for i in range(count - 1)]
    backward = [(i + 1, i) for i in range(count - 1)]

    odd = (lax.axis_index("orb") & 1).astype(jnp.int32).reshape(1)
    even_pair, odd_pair = edges(odd, occupied, virtual, occupied_mask, virtual_mask)
    source, even_pair, odd_pair = lax.optimization_barrier((tensor, even_pair, odd_pair))
    swaps = [[], []]
    for i, j in forward:
        swaps[i % 2] += [(i, j), (j, i)]
    odd_pair = lax.ppermute(odd_pair, "orb", swaps[1])
    even_pair = lax.ppermute(even_pair, "orb", swaps[0])
    arrived = []
    for begin, rows in CUTS:
        x, l = cut(source, tensor_mask, begin, rows)
        source, x, l, odd_pair, even_pair = lax.optimization_barrier(
            (source, x, l, odd_pair, even_pair)
        )
        arrived.append((lax.ppermute(x, "orb", forward), lax.ppermute(l, "orb", backward)))

    total, wide, thin = own_terms(
        odd, tensor, tensor_mask, occupied, virtual, occupied_mask, virtual_mask, even_pair, odd_pair
    )
    wide, thin = hold(wide, thin)
    before = [total]
    for (begin, rows), (x, l) in zip(CUTS, arrived, strict=True):
        last = len(before) == len(CUTS)
        before.append(near_sum(wide, thin, x, l, begin, rows, before if last else ()))
    return scattered_sum(before[-1], "orb")


def solution(mesh):
    return jax.shard_map(
        body,
        mesh=mesh,
        in_specs=(
            P("grp", "orb", None),
            P("orb", "grp"),
            P("grp", "orb", None),
            P("grp", "orb", None),
            P("grp", "orb", None),
            P("grp", "orb", None),
        ),
        out_specs=P("orb", "grp"),
        check_vma=False,
    )
```
